128 devices in a mesh: dp: 8 (over y_hi, x), ha: 4 (over z), wa: 4 (over y_lo, core).
Axes of the slice: x: 4, y: 4 (y_hi: 2, y_lo: 2; y = y_hi * 2 + y_lo), z: 4, core: 2. Of those that a mesh axis runs over, the one named last changes fastest.
Arguments:
- query_in: bfloat16 [8, 4, 4, 384, 512], P('dp', 'ha', 'wa'), may hold values from -30 to 30
- key_in: bfloat16 [8, 4, 4, 384, 512], P('dp', 'ha', 'wa'), may hold values from -6 to 6
- value_in: bfloat16 [8, 4, 4, 384, 512], P('dp', 'ha', 'wa'), may hold values from -6 to 6
- grad_out: bfloat16 [8, 4, 4, 384, 3072], P('dp', 'ha', 'wa'), may hold values from -1.5 to 1.5
- out_weight: bfloat16 [512, 3072], P('dp'), may hold values from -0.25 to 0.25
Outputs:
- outcome: bfloat16 [8, 4, 4, 384, 3072], P('dp', 'ha', 'wa')
- query_grad: float32 [8, 4, 4, 384, 512], P('dp', 'ha', 'wa')
- key_grad: float32 [8, 4, 4, 384, 512], P('dp', 'ha', 'wa')
- value_grad: float32 [8, 4, 4, 384, 512], P('dp', 'ha', 'wa')
- weight_grad: float32 [512, 3072], P('dp')
The draws below stay inside these ranges and needn't reach their ends.
All inputs are finite; a program needn't handle non-finite values.
Results may differ from the reference program's by a relative error of at most 0.035.
Values may be sent and summed in bfloat16 or wider, within the bound.
A program may use at most 192 MiB of HBM per device.

```python
import jax
import jax.numpy as jnp
from jax import lax

D = 3072
HEADS = 4
F = 512
TILE = 384
CLIPS = 8
HTILES = 4
WTILES = 4


def key_field(key):
    base_key = jax.random.fold_in(key, 11)
    field_shape = (CLIPS, HTILES, WTILES, TILE, F)
    values_drawn = 1.5 * jax.random.truncated_normal(base_key, -4.0, 4.0, field_shape, jnp.float32)
    return values_drawn


def draw_key_in(key, part):
    return key_field(key).astype(jnp.bfloat16)


def draw_query_in(key, part):
    base_key = jax.random.fold_in(key, 12)
    field_shape = (CLIPS, HTILES, WTILES, TILE, F)
    values_drawn = 1.5 * jax.random.truncated_normal(base_key, -4.0, 4.0, field_shape, jnp.float32)
    return values_drawn.astype(jnp.bfloat16)


def levels(rng, dims, pieces, low, high):
    def one(position, parts):
        draws = jax.random.uniform(jax.random.fold_in(jax.random.fold_in(rng, 6), position), (parts,), jnp.float32, low / len(pieces), high / len(pieces))
        return jnp.repeat(jnp.exp(draws), dims[position] // parts).reshape((-1,) + (1,) * (len(dims) - position - 1))

    level = one(*pieces[0])
    for cut in pieces[1:]:
        level = level * one(*cut)
    return level


def normal_values(stream_key, shape, spread, most, split=(), kind=jnp.bfloat16):
    result = jax.random.normal(stream_key, shape, jnp.float32) * spread
    if len(split) > 0:
        result = levels(stream_key, shape, split, -0.22, 0.18) * result
    return jnp.clip(result, min=-most, max=most).astype(kind)


def setup_inputs(seed: int = 0) -> dict:
    splits = jax.random.split(jax.random.key(seed), 6)
    query_in = draw_query_in(jax.random.fold_in(splits[5], 71), 0)
    key_in = draw_key_in(jax.random.fold_in(splits[5], 71), 0)
    value_in = normal_values(splits[2], (CLIPS, HTILES, WTILES, TILE, F), 1.0, 6.0, ((0, 8), (1, 4), (2, 4)))
    grad_out = normal_values(splits[3], (CLIPS, HTILES, WTILES, TILE, D), 0.25, 1.5, ((0, 8), (1, 4), (2, 4)))
    out_weight = normal_values(splits[4], (F, D), F ** -0.5, 0.25, ((0, 8),))
    return dict(query_in=query_in, key_in=key_in, value_in=value_in, grad_out=grad_out, out_weight=out_weight)


SCALE_POWER = -0.5


def product(pattern, first_op, second_op):
    return jnp.einsum(pattern, first_op.astype(jnp.float32), second_op.astype(jnp.float32))


def stack_window(extended, tile_cols):
    window_parts = []
    for row_off in range(3):
        for col_off in range(3):
            window_parts.append(extended[row_off, col_off:col_off + tile_cols])
    stacked = jnp.stack(window_parts, axis=1)
    return stacked.reshape((tile_cols, 9 * stacked.shape[2]) + stacked.shape[3:])


def window_keep(row_ok, col_ok, tile_cols, tile_len):
    flag_list = []
    for row_off in range(3):
        for col_off in range(3):
            flag_list.append(jnp.logical_and(row_ok[row_off], col_ok[col_off:col_off + tile_cols]))
    stacked = jnp.stack(flag_list, axis=1)
    return jnp.repeat(stacked, tile_len, axis=1)


def spread_window(stacked, tile_cols, tile_len):
    window_parts = stacked.reshape((tile_cols, 3, 3, tile_len) + stacked.shape[2:])
    spread_rows = []
    for row_off in range(3):
        gathered = None
        for col_off in range(3):
            placed = jnp.pad(window_parts[:, row_off, col_off], ((col_off, 2 - col_off), (0, 0), (0, 0)))
            gathered = placed if gathered is None else gathered + placed
        spread_rows.append(gathered)
    return jnp.stack(spread_rows)


def attend_row(query_row, key_ext, value_ext, visible, head_count):
    tile_cols, tile_len, feature_width = query_row.shape
    head_dim = feature_width // head_count
    score_scale = head_dim ** SCALE_POWER
    query_heads = query_row.reshape(tile_cols, tile_len, head_count, head_dim)
    key_heads = stack_window(key_ext, tile_cols).reshape(tile_cols, 9 * tile_len, head_count, head_dim)
    value_heads = stack_window(value_ext, tile_cols).reshape(tile_cols, 9 * tile_len, head_count, head_dim)
    scores = product("jqhd,jkhd->jhqk", query_heads, key_heads) * score_scale
    scores = jnp.where(visible[:, None, None, :], scores, -1e30)
    row_max = jnp.max(scores, axis=-1, keepdims=True)
    log_norm = row_max + jnp.log(jnp.sum(jnp.exp(scores - row_max), axis=-1, keepdims=True))
    soft_probs = jnp.exp(scores - log_norm).astype(jnp.bfloat16)
    attended = product("jhqk,jkhd->jqhd", soft_probs, value_heads)
    attended = attended.reshape(tile_cols, tile_len, feature_width).astype(jnp.bfloat16)
    return attended, soft_probs, log_norm[..., 0]


def query_back(query_row, key_ext, value_ext, attended, grad_attn, soft_probs, head_count, with_keys):
    tile_cols, tile_len, feature_width = query_row.shape
    head_dim = feature_width // head_count
    score_scale = head_dim ** SCALE_POWER
    attended_heads = attended.astype(jnp.float32).reshape(tile_cols, tile_len, head_count, head_dim)
    grad_heads = grad_attn.reshape(tile_cols, tile_len, head_count, head_dim)
    row_delta = jnp.sum(attended_heads * grad_heads.astype(jnp.float32), axis=-1)
    row_delta = jnp.transpose(row_delta, (0, 2, 1))
    value_heads = stack_window(value_ext, tile_cols).reshape(tile_cols, 9 * tile_len, head_count, head_dim)
    prob_grad = product("jqhd,jkhd->jhqk", grad_heads, value_heads)
    score_grad = (soft_probs.astype(jnp.float32) * (prob_grad - row_delta[..., None])).astype(jnp.bfloat16)
    key_heads = stack_window(key_ext, tile_cols).reshape(tile_cols, 9 * tile_len, head_count, head_dim)
    query_grad = product("jhqk,jkhd->jqhd", score_grad, key_heads) * score_scale
    query_grad = query_grad.reshape(tile_cols, tile_len, feature_width)
    if not with_keys:
        return query_grad, row_delta
    query_heads = query_row.reshape(tile_cols, tile_len, head_count, head_dim)
    key_part = (product("jhqk,jqhd->jkhd", score_grad, query_heads) * score_scale).reshape(tile_cols, 9 * tile_len, feature_width)
    value_part = product("jhqk,jqhd->jkhd", soft_probs, grad_heads).reshape(tile_cols, 9 * tile_len, feature_width)
    return query_grad, row_delta, spread_window(key_part, tile_cols, tile_len), spread_window(value_part, tile_cols, tile_len)


def reference(query_in, key_in, value_in, grad_out, out_weight):
    clip_count, tile_rows, tile_cols, tile_len, feature_width = query_in.shape
    model_width = out_weight.shape[1]
    flat_grad = grad_out.reshape(-1, model_width)
    grad_attn = jnp.dot(flat_grad, out_weight.T, preferred_element_type=jnp.float32)
    grad_attn = grad_attn.astype(jnp.bfloat16).reshape(query_in.shape)
    pad_spec = ((1, 1), (1, 1), (0, 0), (0, 0))
    col_index = jnp.arange(tile_cols + 2, dtype=jnp.int32)
    col_ok = jnp.logical_and(col_index >= 1, col_index <= tile_cols)
    row_index_all = jnp.arange(tile_rows + 2, dtype=jnp.int32)
    row_flags = jnp.logical_and(row_index_all >= 1, row_index_all <= tile_rows)

    def one_clip(clip_data):
        queries, keys_clip, values_clip, grads_clip = clip_data
        key_pad = jnp.pad(keys_clip, pad_spec)
        value_pad = jnp.pad(values_clip, pad_spec)
        zero_pad = jnp.zeros(key_pad.shape, jnp.float32)

        def one_row(carried, row_index):
            key_grad_pad, value_grad_pad = carried
            key_ext = lax.dynamic_slice_in_dim(key_pad, row_index, 3, 0)
            value_ext = lax.dynamic_slice_in_dim(value_pad, row_index, 3, 0)
            row_ok = lax.dynamic_slice_in_dim(row_flags, row_index, 3, 0)
            visible = window_keep(row_ok, col_ok, tile_cols, tile_len)
            query_row = lax.dynamic_index_in_dim(queries, row_index, 0, keepdims=False)
            grad_row = lax.dynamic_index_in_dim(grads_clip, row_index, 0, keepdims=False)
            attended, soft_probs, log_norm = attend_row(query_row, key_ext, value_ext, visible, HEADS)
            query_grad, row_delta, key_part, value_part = query_back(query_row, key_ext, value_ext, attended, grad_row, soft_probs, HEADS, True)
            old_keys = lax.dynamic_slice_in_dim(key_grad_pad, row_index, 3, 0)
            key_grad_pad = lax.dynamic_update_slice_in_dim(key_grad_pad, old_keys + key_part, row_index, 0)
            old_values = lax.dynamic_slice_in_dim(value_grad_pad, row_index, 3, 0)
            value_grad_pad = lax.dynamic_update_slice_in_dim(value_grad_pad, old_values + value_part, row_index, 0)
            return (key_grad_pad, value_grad_pad), (attended, query_grad)

        final_pads, row_outputs = lax.scan(one_row, (zero_pad, zero_pad), jnp.arange(tile_rows, dtype=jnp.int32))
        return row_outputs[0], row_outputs[1], final_pads[0][1:-1, 1:-1], final_pads[1][1:-1, 1:-1]

    attended, query_grad, key_grad, value_grad = lax.map(one_clip, (query_in, key_in, value_in, grad_attn))
    flat_attn = attended.reshape(-1, feature_width)
    outcome = jnp.dot(flat_attn, out_weight, preferred_element_type=jnp.float32).astype(jnp.bfloat16)
    outcome = outcome.reshape(clip_count, tile_rows, tile_cols, tile_len, model_width)
    weight_grad = jnp.dot(flat_attn.T, flat_grad, preferred_element_type=jnp.float32)
    return (outcome, query_grad, key_grad, value_grad, weight_grad)
```

```python
import math

import jax
import jax.numpy as jnp
from jax import lax
from jax.experimental import pallas as pl
from jax.experimental.pallas import tpu as pltpu
from jax.sharding import PartitionSpec as P

MESH = pl.DeviceIdType.MESH
BF = jnp.bfloat16
F32 = jnp.float32

TILE, HD, FEAT, D = 384, 128, 512, 3072
HALF, QUART = D // 2, D // 4
SCALE = HD**-0.5
EXP_SCALE = SCALE * math.log2(math.e)


def dot_nn(a, b):
    return lax.dot_general(a, b, (((1,), (0,)), ((), ())), preferred_element_type=F32)


def dot_nt(a, b):
    return lax.dot_general(a, b, (((1,), (1,)), ((), ())), preferred_element_type=F32)


def dot_tn(a, b):
    return lax.dot_general(a, b, (((0,), (0,)), ((), ())), preferred_element_type=F32)


def flip(v):
    return v + 1 - 2 * lax.rem(v, 2)


def unit_index(t, b):
    return 3 * t + b - 1 - lax.rem(t, 2) * (1 - lax.div(t, 2))


N_SEND, N_RECV = 96, 96


def kernel(
    q_in, k_in, v_in, g_in, w_in,
    out_o, dq_o, dk_o, dv_o, wg_o,
    qg, kg, vg, s_ref, sc_ref, m_ref, p_ref, pc_ref, o_acc, linv, ob, dog, dop, delta,
    dq, dk, dv, ys, zs, cs, yr, zr, cr, dqb, dkb, dvb, att, gat, gat_acc, gov, ws, oc,
    acc, tsend, trecv, xs, xa, xb, xr, rsum, y3s, y3r, y4s, y4r, z4s, z4r, fin,
    ssem, rsem, lsem,
):
    dp, z, wa = lax.axis_index("dp"), lax.axis_index("ha"), lax.axis_index("wa")
    x, yh = lax.rem(dp, 4), lax.div(dp, 4)
    c, ylo = lax.rem(wa, 2), lax.div(wa, 2)
    i, j = lax.rem(lax.div(z + 1, 2), 2), lax.rem(lax.div(wa + 1, 2), 2)
    t_me = 2 * i + j
    zp, wp = flip(z), flip(wa)
    peers = {1: (dp, z, wp), 2: (dp, zp, wa), 3: (dp, zp, wp)}
    peer_t = {0: t_me, 1: 2 * i + 1 - j, 2: 2 * (1 - i) + j, 3: 2 * (1 - i) + 1 - j}
    dev_y, dev_z, dev_c = (dp, z, 3 - wa), (dp, 3 - z, wa), (dp, 3 - z, 3 - wa)
    xp_i, xm_i, x2_i = lax.rem(x + 1, 4), lax.rem(x + 3, 4), lax.rem(x + 2, 4)
    dev_xp, dev_xm = (yh * 4 + xp_i, z, wa), (yh * 4 + xm_i, z, wa)
    dev_yi = (lax.rem(dp + 4, 8), z, lax.rem(wa + 2, 4))
    dev_core = peers[1]
    dev_ylo = (dp, z, lax.rem(wa + 2, 4))
    clip_devs = [
        (dp, lax.rem(z + a, 4), lax.rem(wa + b, 4)) for a in range(4) for b in range(4) if a or b
    ]
    fl = 4 * (1 - yh)

    sends = []
    counts = {"s": 0, "r": 0, "l": 0}

    def new(kind, n=1):
        first = counts[kind]
        counts[kind] += n
        return first

    def send(src, dst, dev, r):
        copy = pltpu.make_async_remote_copy(
            src, dst, ssem.at[new("s")], rsem.at[r], device_id=dev, device_id_type=MESH
        )
        copy.start()
        sends.append(copy)

    def local(src, dst, sem):
        pltpu.make_async_copy(src, dst, sem).start()

    def arrived(dst, r):
        pltpu.make_async_copy(dst, dst, rsem.at[r]).wait()

    def cols(n, width=HD):
        return pl.ds(pl.multiple_of(n * width, width), width)

    barrier = pltpu.get_barrier_semaphore()
    neighbours = clip_devs + [dev_xp, dev_xm, dev_yi]
    for dev in neighbours:
        pl.semaphore_signal(barrier, inc=1, device_id=dev, device_id_type=MESH)

    l_g, l_w = new("l"), new("l")
    local(g_in, gov, lsem.at[l_g])
    local(w_in, ws.at[dp], lsem.at[l_w])
    r_k, r_q, r_v = new("r", 4), new("r", 4), new("r", 4)
    local(k_in.at[:, cols(t_me)], kg.at[2 + t_me], rsem.at[r_k + t_me])
    local(q_in.at[:, cols(t_me)], qg.at[t_me], rsem.at[r_q + t_me])
    local(v_in.at[:, cols(t_me)], vg.at[2 + t_me, :, pl.ds(0, HD)], rsem.at[r_v + t_me])
    pl.semaphore_wait(barrier, len(neighbours))

    for n in (2, 3, 1):
        send(k_in.at[:, cols(peer_t[n])], kg.at[2 + t_me], peers[n], r_k + t_me)
    hc = pl.ds(pl.multiple_of(c * HALF, HALF), HALF)
    hca = pl.ds(pl.multiple_of(c * HALF, HALF), QUART)
    hcb = pl.ds(pl.multiple_of(c * HALF + QUART, QUART), QUART)
    hall = pl.ds(0, 64)
    r_w = new("r", 8)
    r_wc = new("r", 7)
    send(w_in.at[hall, hc], ws.at[dp, hall, hc], dev_xp, r_w + 0)
    send(w_in.at[hall, hc], ws.at[dp, hall, hc], dev_xm, r_w + 1)
    send(w_in.at[hall, hc], ws.at[dp, hall, hc], dev_yi, r_w + 2)
    for n in (2, 3, 1):
        send(q_in.at[:, cols(peer_t[n])], qg.at[t_me], peers[n], r_q + t_me)
    for n in (2, 3, 1):
        send(v_in.at[:, cols(peer_t[n])], vg.at[2 + t_me, :, pl.ds(0, HD)], peers[n], r_v + t_me)

    def ones(s, _):
        vg[s, :, HD:] = jnp.ones((TILE, HD), BF)
        return 0

    lax.fori_loop(0, 9, ones, 0)
    m_ref[...] = jnp.full(m_ref.shape, -jnp.inf, F32)
    dq[...] = jnp.zeros(dq.shape, F32)
    dk[...] = jnp.zeros(dk.shape, F32)
    dv[...] = jnp.zeros(dv.shape, F32)

    def halo_of(buf, r_own, width, r_halo):
        def at(s):
            return buf.at[s] if width is None else buf.at[s, :, pl.ds(0, width)]

        for s in (3, 5, 4, 2):
            arrived(at(s), r_own + s - 2)
            if s == 3:
                send(at(3), at(6), dev_y, r_halo + 2)
            if s == 5:
                send(at(5), at(7), dev_y, r_halo + 3)
                send(at(5), at(1), dev_z, r_halo + 1)
                send(at(5), at(8), dev_c, r_halo + 4)
            if s == 4:
                send(at(4), at(0), dev_z, r_halo + 0)

    def w_at(d, columns):
        return ws.at[d, hall, columns]

    d_xm, d_xp, d_x2 = yh * 4 + xm_i, yh * 4 + xp_i, yh * 4 + x2_i
    f_x, f_xm, f_xp, f_x2 = fl + x, fl + xm_i, fl + xp_i, fl + x2_i

    r_kh, r_vh = new("r", 5), new("r", 5)
    halo_of(kg, r_k, None, r_kh)

    arrived(w_at(d_xm, hc), r_w + 0)
    send(w_at(d_xm, hca), w_at(d_xm, hca), dev_xp, r_w + 3)
    send(w_at(d_xm, hc), w_at(d_xm, hc), dev_core, r_wc + 0)
    arrived(w_at(d_xp, hc), r_w + 1)
    send(w_at(d_xp, hcb), w_at(d_xp, hcb), dev_xm, r_w + 4)
    send(w_at(d_xp, hc), w_at(d_xp, hc), dev_core, r_wc + 1)
    arrived(w_at(f_x, hc), r_w + 2)
    send(w_at(f_x, hc), w_at(f_x, hc), dev_xp, r_w + 5)
    send(w_at(f_x, hc), w_at(f_x, hc), dev_xm, r_w + 6)
    send(w_at(f_x, hc), w_at(f_x, hc), dev_core, r_wc + 2)

    for s in range(4):
        arrived(qg.at[s], r_q + s)

    def scores(t, b):
        s = dot_nt(qg[t], kg[pl.ds(2 * b, 2)].reshape(2 * TILE, HD))
        s_ref[unit_index(t, b)] = s
        m = m_ref[t]
        for n in range(6):
            m = jnp.maximum(m, s[:, n * HD : (n + 1) * HD])
        m_ref[t] = m

    def own_scores(n, _):
        scores(lax.div(n, 2), 1 + lax.rem(n, 2))
        return 0

    lax.fori_loop(0, 8, own_scores, 0)

    arrived(w_at(d_x2, hca), r_w + 3)
    arrived(w_at(d_x2, hcb), r_w + 4)
    send(w_at(d_x2, hc), w_at(d_x2, hc), dev_yi, r_w + 7)
    send(w_at(d_x2, hc), w_at(d_x2, hc), dev_core, r_wc + 3)

    for s, r in ((0, 0), (1, 1), (6, 2), (7, 3), (8, 4)):
        arrived(kg.at[s], r_kh + r)

    def halo_scores(n, _):
        late = lax.div(n, 2)
        scores(jnp.where(late == 0, 1 + 2 * n, n), 3 - 3 * late)
        return 0

    lax.fori_loop(0, 4, halo_scores, 0)
    s = dot_nt(qg[3], kg[8])
    sc_ref[...] = s
    m_ref[3] = jnp.maximum(
        jnp.maximum(m_ref[3], s[:, :HD]), jnp.maximum(s[:, HD : 2 * HD], s[:, 2 * HD :])
    )

    halo_of(vg, r_v, HD, r_vh)

    def weigh(t, low, high):
        m = jnp.max(m_ref[t], axis=-1, keepdims=True) * EXP_SCALE

        def block(b, _):
            u = unit_index(t, b)
            p = jnp.exp2(s_ref[u] * EXP_SCALE - m).astype(BF)
            p_ref[u] = p
            o_acc[...] += dot_nn(p, vg[pl.ds(2 * b, 2)].reshape(2 * TILE, 2 * HD))
            return 0

        o_acc[...] = jnp.zeros(o_acc.shape, F32)
        lax.fori_loop(low, high, block, 0)
        return m

    def attend(t):
        inverse = 1.0 / o_acc[:, HD:]
        linv[t] = inverse
        ob[t] = (o_acc[:, :HD] * inverse).astype(BF)

    t0 = jnp.int32(0)
    weigh(t0, 1, 3)
    attend(t0)

    arrived(w_at(f_xm, hc), r_w + 5)
    send(w_at(f_xm, hc), w_at(f_xm, hc), dev_core, r_wc + 4)
    arrived(w_at(f_xp, hc), r_w + 6)
    send(w_at(f_xp, hc), w_at(f_xp, hc), dev_core, r_wc + 5)
    arrived(w_at(f_x2, hc), r_w + 7)
    send(w_at(f_x2, hc), w_at(f_x2, hc), dev_core, r_wc + 6)

    for s, r in ((0, 0), (1, 1), (6, 2), (7, 3), (8, 4)):
        arrived(vg.at[s, :, pl.ds(0, HD)], r_vh + r)
    weigh(t0 + 1, 1, 4)
    attend(t0 + 1)
    weigh(t0 + 2, 0, 3)
    attend(t0 + 2)
    m = weigh(t0 + 3, 0, 4)
    p = jnp.exp2(sc_ref[...] * EXP_SCALE - m).astype(BF)
    pc_ref[...] = p
    o_acc[...] += dot_nn(p, vg[8])
    attend(t0 + 3)

    r_o = new("r", 4)
    local(ob.at[t_me], att.at[:, cols(t_me)], rsem.at[r_o + t_me])
    for n in (2, 3, 1):
        send(ob.at[peer_t[n]], att.at[:, cols(t_me)], peers[n], r_o + t_me)

    pltpu.make_async_copy(g_in, gov, lsem.at[l_g]).wait()
    pltpu.make_async_copy(w_in, ws.at[dp], lsem.at[l_w]).wait()
    hc_o = pl.ds(pl.multiple_of((1 - c) * HALF, HALF), HALF)
    for n, d in enumerate((d_xm, d_xp, f_x, d_x2, f_xm, f_xp, f_x2)):
        arrived(w_at(d, hc_o), r_wc + n)
    gat_acc[...] = jnp.zeros(gat_acc.shape, F32)

    def grad_block(n, _):
        wide = pl.ds(pl.multiple_of(n * 512, 512), 512)
        gat_acc[...] += dot_nt(gov[:, wide], ws[:, :, wide].reshape(FEAT, 512))
        return 0

    lax.fori_loop(0, 6, grad_block, 0)
    gat[...] = gat_acc[...].astype(BF)
    r_g = new("r", 4)
    local(gat.at[:, cols(t_me)], dog.at[t_me], rsem.at[r_g + t_me])
    for n in (2, 3, 1):
        send(gat.at[:, cols(peer_t[n])], dog.at[t_me], peers[n], r_g + t_me)

    for s in range(4):
        arrived(att.at[:, cols(s)], r_o + s)

    def term_block(n, into, half):
        wide = pl.ds(pl.multiple_of(half * HALF + n * 512, 512), 512)
        to = pl.ds(pl.multiple_of(n * 512, 512), 512)
        d = dot_tn(att[...], gov[:, wide])
        for h in range(2):
            for xx in range(4):
                first = h * 256 + xx * 64
                into[xx, h, :, to] = d[first : first + 64].astype(into.dtype)

    def other_half(n, _):
        term_block(n, tsend, 1 - c)
        return 0

    def own_half(n, _):
        term_block(n, acc, c)
        return 0

    lax.fori_loop(0, 3, other_half, 0)
    r_t = new("r")
    send(tsend, trecv, dev_core, r_t)
    lax.fori_loop(0, 3, own_half, 0)

    arrived(trecv, r_t)

    def add_core(n, _):
        s = acc[n] + trecv[n].astype(F32)
        acc[n] = s
        xs[n] = s.astype(BF)
        return 0

    lax.fori_loop(0, 4, add_core, 0)
    two, rows = pl.ds(0, 2), pl.ds(0, 64)
    ca, cb = pl.ds(0, QUART), pl.ds(QUART, QUART)
    r_xa, r_xr = new("r", 2), new("r", 4)
    send(xs.at[x2_i, two, rows, ca], xa.at[0], dev_xp, r_xa)
    send(xs.at[x2_i, two, rows, cb], xa.at[1], dev_xm, r_xa + 1)
    send(xs.at[xp_i, two, rows, cb], xr.at[2], dev_xp, r_xr + 2)
    send(xs.at[xm_i, two, rows, ca], xr.at[3], dev_xm, r_xr + 3)

    for s in range(4):
        arrived(dog.at[s], r_g + s)

    def prepare(t, _):
        scaled = (dog[t].astype(F32) * linv[t]).astype(BF)
        dop[t] = scaled
        d = jnp.sum(ob[t].astype(F32) * scaled.astype(F32), axis=-1, keepdims=True)
        delta[t] = jnp.broadcast_to(d, (TILE, HD))
        return 0

    lax.fori_loop(0, 4, prepare, 0)

    def back(t, b):
        p = p_ref[unit_index(t, b)]
        keys = kg[pl.ds(2 * b, 2)].reshape(2 * TILE, HD)
        values = vg[pl.ds(2 * b, 2), :, :HD].reshape(2 * TILE, HD)
        dprob = dot_nt(dop[t], values)
        ds = (p.astype(F32) * (dprob - delta[t][:, :1])).astype(BF)
        dq[t] += dot_nn(ds, keys)
        dk[b] += dot_tn(ds, qg[t])
        dv[b] += dot_tn(p, dop[t])

    p = pc_ref[...]
    dprob = dot_nt(dop[3], vg[8, :, :HD])
    ds = (p.astype(F32) * (dprob - delta[3][:, :1])).astype(BF)
    dq[3] += dot_nn(ds, kg[8])
    cs[0] = (dot_tn(ds, qg[3]) * SCALE).astype(BF)
    cs[1] = dot_tn(p, dop[3]).astype(BF)
    r_cb, r_yb, r_zb = new("r"), new("r"), new("r")
    send(cs, cr, dev_c, r_cb)

    def back_y(n, _):
        back(1 + 2 * n, jnp.int32(3))
        return 0

    lax.fori_loop(0, 2, back_y, 0)
    ys[0] = (dk[3] * SCALE).astype(BF)
    ys[1] = dv[3].astype(BF)
    send(ys, yr, dev_y, r_yb)

    def back_z(n, _):
        back(2 + n, jnp.int32(0))
        return 0

    lax.fori_loop(0, 2, back_z, 0)
    zs[0] = (dk[0] * SCALE).astype(BF)
    zs[1] = dv[0].astype(BF)
    send(zs, zr, dev_z, r_zb)

    arrived(xa.at[0], r_xa)
    xb[0] = (acc[xp_i, :, :, :QUART] + xa[0].astype(F32)).astype(BF)
    send(xb.at[0], xr.at[0], dev_xp, r_xr + 0)
    arrived(xa.at[1], r_xa + 1)
    xb[1] = (acc[xm_i, :, :, QUART:] + xa[1].astype(F32)).astype(BF)
    send(xb.at[1], xr.at[1], dev_xm, r_xr + 1)

    def back_own(n, _):
        back(lax.rem(n, 4), 1 + lax.div(n, 4))
        return 0

    lax.fori_loop(0, 8, back_own, 0)

    dqb[...] = (dq[...] * SCALE).astype(BF)
    r_dq, r_dk, r_dv = new("r", 4), new("r", 4), new("r", 4)

    def give(buf, out, r):
        local(buf.at[t_me], out.at[:, cols(t_me)], rsem.at[r + t_me])
        for n in (2, 3, 1):
            send(buf.at[peer_t[n]], out.at[:, cols(t_me)], peers[n], r + t_me)

    give(dqb, dq_o, r_dq)

    for n in range(4):
        arrived(xr.at[n], r_xr + n)
    rsum[:, :, :QUART] = acc[x, :, :, :QUART] + xr[0].astype(F32) + xr[3].astype(F32)
    rsum[:, :, QUART:] = acc[x, :, :, QUART:] + xr[1].astype(F32) + xr[2].astype(F32)
    y3s[...] = rsum[1 - yh].astype(BF)
    r_3 = new("r")
    send(y3s, y3r, dev_yi, r_3)

    arrived(cr, r_cb)
    arrived(yr, r_yb)
    arrived(zr, r_zb)
    for n, (own, fin_b, sc) in enumerate(((dk, dkb, SCALE), (dv, dvb, 1.0))):
        fin_b[0] = (own[1, :TILE] * sc).astype(BF)
        fin_b[1] = (own[1, TILE:] * sc + yr[n, :TILE].astype(F32)).astype(BF)
        fin_b[2] = (own[2, :TILE] * sc + zr[n, :TILE].astype(F32)).astype(BF)
        fin_b[3] = (
            own[2, TILE:] * sc + yr[n, TILE:].astype(F32) + zr[n, TILE:].astype(F32)
            + cr[n].astype(F32)
        ).astype(BF)
    give(dkb, dk_o, r_dk)
    give(dvb, dv_o, r_dv)

    arrived(y3r, r_3)
    half_o = pl.ds(pl.multiple_of((1 - ylo) * QUART, QUART), QUART)
    half_m = pl.ds(pl.multiple_of(ylo * QUART, QUART), QUART)
    y4s[...] = (rsum[yh, :, half_o] + y3r[:, half_o].astype(F32)).astype(BF)
    r_4 = new("r")
    send(y4s, y4r, dev_ylo, r_4)

    l_o = new("l", 6)

    def project(n):
        wide = pl.ds(n * 512, 512)
        oc[:, wide] = dot_nn(att[...], ws[:, :, wide].reshape(FEAT, 512)).astype(BF)
        local(oc.at[:, wide], out_o.at[:, wide], lsem.at[l_o + n])

    for n in range(3):
        project(n)
    arrived(y4r, r_4)
    z4s[...] = (rsum[yh, :, half_m] + y3r[:, half_m].astype(F32) + y4r[...].astype(F32)).astype(BF)
    r_z4 = new("r", 3)
    for n in (1, 2, 3):
        to = lax.rem(z + n, 4)
        some = pl.ds(pl.multiple_of(to * 16, 16), 16)
        send(z4s.at[some, pl.ds(0, QUART)], z4r.at[n - 1], (dp, to, wa), r_z4 + n - 1)
    for n in range(3, 6):
        project(n)
    mine = pl.ds(pl.multiple_of(z * 16, 16), 16)
    total = rsum[yh, mine, half_m] + y3r[mine, half_m].astype(F32) + y4r[mine, :].astype(F32)
    for n in range(3):
        arrived(z4r.at[n], r_z4 + n)
        total += z4r[n].astype(F32)
    fin[...] = total.astype(BF)
    place = wg_o.at[mine, pl.ds(pl.multiple_of(c * HALF + ylo * QUART, QUART), QUART)]
    r_f = new("r", 16)
    n = 0
    for a in range(4):
        for b in range(4):
            if a == 0 and b == 0:
                local(fin, place, rsem.at[r_f])
            else:
                dev = (dp, lax.rem(z + a, 4), lax.rem(wa + b, 4))
                send(fin, place, dev, r_f + n)
            n += 1

    for r, out in ((r_dq, dq_o), (r_dk, dk_o), (r_dv, dv_o)):
        for s in range(4):
            arrived(out.at[:, cols(s)], r + s)
    for n in range(6):
        wide = pl.ds(n * 512, 512)
        pltpu.make_async_copy(oc.at[:, wide], out_o.at[:, wide], lsem.at[l_o + n]).wait()
    for n in range(16):
        arrived(place, r_f + n)
    for copy in sends:
        copy.wait_send()
    assert counts["s"] <= N_SEND and counts["r"] <= N_RECV, counts


def on_device(q, k, v, g, w):
    def vm(*shape, dtype=BF):
        return pltpu.VMEM(shape, dtype)

    def f(*shape):
        return pltpu.VMEM(shape, F32)

    any_spec = pl.BlockSpec(memory_space=pl.ANY)
    tile = jax.ShapeDtypeStruct((TILE, FEAT), BF)
    outs = pl.pallas_call(
        kernel,
        out_shape=(
            jax.ShapeDtypeStruct((TILE, D), BF), tile, tile, tile,
            jax.ShapeDtypeStruct((64, D), BF),
        ),
        in_specs=[any_spec] * 5,
        out_specs=[any_spec] * 5,
        scratch_shapes=[
            vm(4, TILE, HD), vm(9, TILE, HD), vm(9, TILE, 2 * HD),
            f(12, TILE, 2 * TILE), f(TILE, TILE), f(4, TILE, HD),
            vm(12, TILE, 2 * TILE), vm(TILE, TILE), f(TILE, 2 * HD),
            f(4, TILE, HD), vm(4, TILE, HD), vm(4, TILE, HD), vm(4, TILE, HD), f(4, TILE, HD),
            f(4, TILE, HD), f(4, 2 * TILE, HD), f(4, 2 * TILE, HD),
                vm(2, 2 * TILE, HD), vm(2, 2 * TILE, HD), vm(2, TILE, HD),
            vm(2, 2 * TILE, HD), vm(2, 2 * TILE, HD), vm(2, TILE, HD),
            vm(4, TILE, HD), vm(4, TILE, HD), vm(4, TILE, HD),
            vm(TILE, FEAT), vm(TILE, FEAT), f(TILE, FEAT),
            vm(TILE, D), vm(8, 64, D), vm(TILE, D),
            f(4, 2, 64, HALF), vm(4, 2, 64, HALF), vm(4, 2, 64, HALF), vm(4, 2, 64, HALF),
            vm(2, 2, 64, QUART), vm(2, 2, 64, QUART), vm(4, 2, 64, QUART),
            f(2, 64, HALF), vm(64, HALF), vm(64, HALF),
            vm(64, QUART), vm(64, QUART), vm(64, QUART), vm(3, 16, QUART), vm(16, QUART),
            pltpu.SemaphoreType.DMA((N_SEND,)),
            pltpu.SemaphoreType.DMA((N_RECV,)),
            pltpu.SemaphoreType.DMA((8,)),
        ],
        compiler_params=pltpu.CompilerParams(
            collective_id=0, has_side_effects=True, vmem_limit_bytes=60 << 20
        ),
        name="sublayer",
    )(
        q.reshape(TILE, FEAT), k.reshape(TILE, FEAT), v.reshape(TILE, FEAT), g.reshape(TILE, D), w
    )
    outcome, dq, dk, dv, wg = outs
    return (
        outcome.reshape(g.shape),
        dq.astype(F32).reshape(q.shape),
        dk.astype(F32).reshape(q.shape),
        dv.astype(F32).reshape(q.shape),
        wg.astype(F32),
    )


def solution(mesh):
    tiles = P("dp", "ha", "wa", None, None)
    return jax.shard_map(
        on_device,
        mesh=mesh,
        in_specs=(tiles, tiles, tiles, tiles, P("dp", None)),
        out_specs=(tiles, tiles, tiles, tiles, P("dp", None)),
        check_vma=False,
    )
```

```python
import math

import jax
import jax.numpy as jnp
from jax import lax
from jax.experimental import pallas as pl
from jax.experimental.pallas import tpu as pltpu
from jax.sharding import PartitionSpec as P

MESH = pl.DeviceIdType.MESH
BF = jnp.bfloat16
F32 = jnp.float32

TILE, HD, FEAT, D = 384, 128, 512, 3072
HALF, QUART = D // 2, D // 4
SCALE = HD**-0.5
EXP_SCALE = SCALE * math.log2(math.e)


def dot_nn(a, b):
    return lax.dot_general(a, b, (((1,), (0,)), ((), ())), preferred_element_type=F32)


def dot_nt(a, b):
    return lax.dot_general(a, b, (((1,), (1,)), ((), ())), preferred_element_type=F32)


def dot_tn(a, b):
    return lax.dot_general(a, b, (((0,), (0,)), ((), ())), preferred_element_type=F32)


def flip(v):
    return v + 1 - 2 * lax.rem(v, 2)


def unit_index(t, b):
    return 3 * t + b - 1 - lax.rem(t, 2) * (1 - lax.div(t, 2))


N_SEND, N_RECV, N_LOCAL = 128, 128, 16


def kernel(
    q_in, k_in, v_in, g_in, w_in,
    out_o, dq_o, dk_o, dv_o, wg_o,
    qg, kg, vg, s_ref, sc_ref, m_ref, p_ref, pc_ref, o_acc, linv, ob, dog, dop, delta,
    dq, dk, dv, ys, zs, cs, yr, zr, cr, dqb, dkb, dvb, dqr, dkr, dvr, att, gat, gat_acc, gov, g2, ws, oc,
    acc, xs, xa, xb, xr, rsum, y3s, y3r, y4s, y4r, z4s, z4r, fin, wgr,
    ssem, rsem, lsem,
):
    dp, z, wa = lax.axis_index("dp"), lax.axis_index("ha"), lax.axis_index("wa")
    x, yh = lax.rem(dp, 4), lax.div(dp, 4)
    c, ylo = lax.rem(wa, 2), lax.div(wa, 2)
    i, j = lax.rem(lax.div(z + 1, 2), 2), lax.rem(lax.div(wa + 1, 2), 2)
    t_me = 2 * i + j
    zp, wp = flip(z), flip(wa)
    peers = {1: (dp, z, wp), 2: (dp, zp, wa), 3: (dp, zp, wp)}
    peer_t = {0: t_me, 1: 2 * i + 1 - j, 2: 2 * (1 - i) + j, 3: 2 * (1 - i) + 1 - j}
    dev_y, dev_z, dev_c = (dp, z, 3 - wa), (dp, 3 - z, wa), (dp, 3 - z, 3 - wa)
    xp_i, xm_i, x2_i = lax.rem(x + 1, 4), lax.rem(x + 3, 4), lax.rem(x + 2, 4)
    dev_xp, dev_xm = (yh * 4 + xp_i, z, wa), (yh * 4 + xm_i, z, wa)
    dev_yi = (lax.rem(dp + 4, 8), z, lax.rem(wa + 2, 4))
    dev_core = peers[1]
    dev_ylo = (dp, z, lax.rem(wa + 2, 4))
    clip_devs = [
        (dp, lax.rem(z + a, 4), lax.rem(wa + b, 4)) for a in range(4) for b in range(4) if a or b
    ]
    fl = 4 * (1 - yh)

    sends = []
    counts = {"s": 0, "r": 0, "l": 0}

    def new(kind, n=1):
        first = counts[kind]
        counts[kind] += n
        return first

    def send(src, dst, dev, r):
        copy = pltpu.make_async_remote_copy(
            src, dst, ssem.at[new("s")], rsem.at[r], device_id=dev, device_id_type=MESH
        )
        copy.start()
        sends.append(copy)

    def local(src, dst, sem):
        pltpu.make_async_copy(src, dst, sem).start()

    def arrived(dst, r):
        pltpu.make_async_copy(dst, dst, rsem.at[r]).wait()

    def cols(n, width=HD):
        return pl.ds(pl.multiple_of(n * width, width), width)

    barrier = pltpu.get_barrier_semaphore()
    neighbours = clip_devs + [dev_xp, dev_xm, dev_yi]
    for dev in neighbours:
        pl.semaphore_signal(barrier, inc=1, device_id=dev, device_id_type=MESH)

    l_g, l_w = new("l"), new("l")
    local(g_in, gov, lsem.at[l_g])
    l_h = new("l")
    local(g_in.at[:, pl.ds(pl.multiple_of(c * HALF, HALF), HALF)], g2.at[0], lsem.at[l_h])
    local(w_in, ws.at[dp], lsem.at[l_w])
    r_k, r_q, r_v = new("r", 4), new("r", 4), new("r", 4)
    local(k_in.at[:, cols(t_me)], kg.at[2 + t_me], rsem.at[r_k + t_me])
    local(q_in.at[:, cols(t_me)], qg.at[t_me], rsem.at[r_q + t_me])
    local(v_in.at[:, cols(t_me)], vg.at[2 + t_me, :, pl.ds(0, HD)], rsem.at[r_v + t_me])
    pl.semaphore_wait(barrier, len(neighbours))

    for n in (2, 3, 1):
        send(k_in.at[:, cols(peer_t[n])], kg.at[2 + t_me], peers[n], r_k + t_me)
    hc = pl.ds(pl.multiple_of(c * HALF, HALF), HALF)
    hca = pl.ds(pl.multiple_of(c * HALF, HALF), QUART)
    hcb = pl.ds(pl.multiple_of(c * HALF + QUART, QUART), QUART)
    hall = pl.ds(0, 64)
    r_w = new("r", 8)
    r_wc = new("r", 7)
    send(w_in.at[hall, hc], ws.at[dp, hall, hc], dev_xp, r_w + 0)
    send(w_in.at[hall, hc], ws.at[dp, hall, hc], dev_xm, r_w + 1)
    send(w_in.at[hall, hc], ws.at[dp, hall, hc], dev_yi, r_w + 2)
    for n in (2, 3, 1):
        send(q_in.at[:, cols(peer_t[n])], qg.at[t_me], peers[n], r_q + t_me)
    for n in (2, 3, 1):
        send(v_in.at[:, cols(peer_t[n])], vg.at[2 + t_me, :, pl.ds(0, HD)], peers[n], r_v + t_me)

    r_gx = new("r")
    hc_o = pl.ds(pl.multiple_of((1 - c) * HALF, HALF), HALF)
    send(g_in.at[:, hc_o], g2.at[1], dev_core, r_gx)

    def ones(s, _):
        vg[s, :, HD:] = jnp.ones((TILE, HD), BF)
        return 0

    lax.fori_loop(0, 9, ones, 0)
    m_ref[...] = jnp.full(m_ref.shape, -jnp.inf, F32)
    dq[...] = jnp.zeros(dq.shape, F32)
    dk[...] = jnp.zeros(dk.shape, F32)
    dv[...] = jnp.zeros(dv.shape, F32)
    o_acc[...] = jnp.zeros(o_acc.shape, F32)

    def halo_of(buf, r_own, width, r_halo):
        def at(s):
            return buf.at[s] if width is None else buf.at[s, :, pl.ds(0, width)]

        for s in (3, 5, 4, 2):
            arrived(at(s), r_own + s - 2)
            if s == 3:
                send(at(3), at(6), dev_y, r_halo + 2)
            if s == 5:
                send(at(5), at(7), dev_y, r_halo + 3)
                send(at(5), at(1), dev_z, r_halo + 1)
                send(at(5), at(8), dev_c, r_halo + 4)
            if s == 4:
                send(at(4), at(0), dev_z, r_halo + 0)

    def w_at(d, columns):
        return ws.at[d, hall, columns]

    d_xm, d_xp, d_x2 = yh * 4 + xm_i, yh * 4 + xp_i, yh * 4 + x2_i
    f_x, f_xm, f_xp, f_x2 = fl + x, fl + xm_i, fl + xp_i, fl + x2_i

    r_kh, r_vh = new("r", 5), new("r", 5)
    halo_of(kg, r_k, None, r_kh)

    arrived(w_at(d_xm, hc), r_w + 0)
    send(w_at(d_xm, hca), w_at(d_xm, hca), dev_xp, r_w + 3)
    send(w_at(d_xm, hc), w_at(d_xm, hc), dev_core, r_wc + 0)
    arrived(w_at(d_xp, hc), r_w + 1)
    send(w_at(d_xp, hcb), w_at(d_xp, hcb), dev_xm, r_w + 4)
    send(w_at(d_xp, hc), w_at(d_xp, hc), dev_core, r_wc + 1)
    arrived(w_at(f_x, hc), r_w + 2)
    send(w_at(f_x, hc), w_at(f_x, hc), dev_xp, r_w + 5)
    send(w_at(f_x, hc), w_at(f_x, hc), dev_xm, r_w + 6)
    send(w_at(f_x, hc), w_at(f_x, hc), dev_core, r_wc + 2)

    for s in range(4):
        arrived(qg.at[s], r_q + s)
    arrived(w_at(d_x2, hca), r_w + 3)
    arrived(w_at(d_x2, hcb), r_w + 4)
    send(w_at(d_x2, hc), w_at(d_x2, hc), dev_yi, r_w + 7)
    send(w_at(d_x2, hc), w_at(d_x2, hc), dev_core, r_wc + 3)

    def scores(t, b):
        s = dot_nt(qg[t], kg[pl.ds(2 * b, 2)].reshape(2 * TILE, HD))
        s_ref[unit_index(t, b)] = s
        m = m_ref[t]
        for n in range(6):
            m = jnp.maximum(m, s[:, n * HD : (n + 1) * HD])
        m_ref[t] = m

    def own_scores(n, _):
        scores(lax.div(n, 2), 1 + lax.rem(n, 2))
        return 0

    lax.fori_loop(0, 8, own_scores, 0)

    for s, r in ((0, 0), (1, 1), (6, 2), (7, 3), (8, 4)):
        arrived(kg.at[s], r_kh + r)

    def halo_scores(n, _):
        late = lax.div(n, 2)
        scores(jnp.where(late == 0, 1 + 2 * n, n), 3 - 3 * late)
        return 0

    lax.fori_loop(0, 4, halo_scores, 0)
    s = dot_nt(qg[3], kg[8])
    sc_ref[...] = s
    m_ref[3] = jnp.maximum(
        jnp.maximum(m_ref[3], s[:, :HD]), jnp.maximum(s[:, HD : 2 * HD], s[:, 2 * HD :])
    )

    halo_of(vg, r_v, HD, r_vh)

    arrived(w_at(f_xm, hc), r_w + 5)
    send(w_at(f_xm, hc), w_at(f_xm, hc), dev_core, r_wc + 4)
    arrived(w_at(f_xp, hc), r_w + 6)
    send(w_at(f_xp, hc), w_at(f_xp, hc), dev_core, r_wc + 5)

    def row_max(t, _):
        m = jnp.max(m_ref[t], axis=-1, keepdims=True) * EXP_SCALE
        m_ref[t] = jnp.broadcast_to(m, (TILE, HD))
        return 0

    lax.fori_loop(0, 4, row_max, 0)

    def weigh(t, b):
        u = unit_index(t, b)
        p = jnp.exp2(s_ref[u] * EXP_SCALE - m_ref[t][:, :1]).astype(BF)
        p_ref[u] = p
        o_acc[t] += dot_nn(p, vg[pl.ds(2 * b, 2)].reshape(2 * TILE, 2 * HD))

    def weigh_own(n, _):
        weigh(lax.div(n, 2), 1 + lax.rem(n, 2))
        return 0

    lax.fori_loop(0, 4, weigh_own, 0)
    arrived(w_at(f_x2, hc), r_w + 7)
    send(w_at(f_x2, hc), w_at(f_x2, hc), dev_core, r_wc + 6)
    lax.fori_loop(4, 6, weigh_own, 0)

    pltpu.make_async_copy(g_in, gov, lsem.at[l_g]).wait()
    pltpu.make_async_copy(w_in, ws.at[dp], lsem.at[l_w]).wait()
    for n, d in enumerate((d_xm, d_xp, f_x, d_x2, f_xm, f_xp, f_x2)):
        arrived(w_at(d, hc_o), r_wc + n)
    gat_acc[...] = jnp.zeros(gat_acc.shape, F32)

    def grad_block(n, _):
        wide = pl.ds(pl.multiple_of(n * 512, 512), 512)
        gat_acc[...] += dot_nt(gov[:, wide], ws[:, :, wide].reshape(FEAT, 512))
        return 0

    lax.fori_loop(0, 6, grad_block, 0)
    gat[...] = gat_acc[...].astype(BF)
    r_g = new("r", 4)
    for n in (2, 3, 1):
        send(gat.at[:, cols(peer_t[n])], dog.at[t_me], peers[n], r_g + t_me)
    local(gat.at[:, cols(t_me)], dog.at[t_me], rsem.at[r_g + t_me])

    lax.fori_loop(6, 8, weigh_own, 0)
    for s, r in ((0, 0), (1, 1), (6, 2), (7, 3), (8, 4)):
        arrived(vg.at[s, :, pl.ds(0, HD)], r_vh + r)

    def weigh_halo(n, _):
        late = lax.div(n, 2)
        weigh(jnp.where(late == 0, 1 + 2 * n, n), 3 - 3 * late)
        return 0

    lax.fori_loop(0, 4, weigh_halo, 0)
    p = jnp.exp2(sc_ref[...] * EXP_SCALE - m_ref[3][:, :1]).astype(BF)
    pc_ref[...] = p
    o_acc[3] += dot_nn(p, vg[8])

    r_o = new("r", 4)
    for n in (2, 3, 1, 0):
        t = peer_t[n]
        inverse = 1.0 / o_acc[t, :, HD:]
        linv[t] = inverse
        ob[t] = (o_acc[t, :, :HD] * inverse).astype(BF)
        if n:
            send(ob.at[t], att.at[0, :, cols(t_me)], peers[n], r_o + t_me)
        else:
            local(ob.at[t], att.at[0, :, cols(t_me)], rsem.at[r_o + t_me])

    for s in range(4):
        arrived(dog.at[s], r_g + s)

    def prepare(t, _):
        scaled = (dog[t].astype(F32) * linv[t]).astype(BF)
        dop[t] = scaled
        d = jnp.sum(ob[t].astype(F32) * scaled.astype(F32), axis=-1, keepdims=True)
        delta[t] = jnp.broadcast_to(d, (TILE, HD))
        return 0

    lax.fori_loop(0, 4, prepare, 0)

    def back(t, b):
        p = p_ref[unit_index(t, b)]
        keys = kg[pl.ds(2 * b, 2)].reshape(2 * TILE, HD)
        values = vg[pl.ds(2 * b, 2), :, :HD].reshape(2 * TILE, HD)
        dprob = dot_nt(dop[t], values)
        ds = (p.astype(F32) * (dprob - delta[t][:, :1])).astype(BF)
        dq[t] += dot_nn(ds, keys)
        dk[b] += dot_tn(ds, qg[t])
        dv[b] += dot_tn(p, dop[t])

    def back_y(n, _):
        back(1 + 2 * n, jnp.int32(3))
        return 0

    def back_z(n, _):
        back(2 + n, jnp.int32(0))
        return 0

    r_cb, r_yb, r_zb = new("r"), new("r"), new("r")
    p = pc_ref[...]
    dprob = dot_nt(dop[3], vg[8, :, :HD])
    ds = (p.astype(F32) * (dprob - delta[3][:, :1])).astype(BF)
    dq[3] += dot_nn(ds, kg[8])
    cs[0] = dot_tn(ds, qg[3]).astype(BF)
    cs[1] = dot_tn(p, dop[3]).astype(BF)
    send(cs, cr, dev_c, r_cb)

    lax.fori_loop(0, 2, back_y, 0)
    ys[0] = dk[3].astype(BF)
    ys[1] = dv[3].astype(BF)
    send(ys, yr, dev_y, r_yb)
    lax.fori_loop(0, 1, back_z, 0)

    for s in range(4):
        arrived(att.at[0, :, cols(s)], r_o + s)
    r_a = new("r")
    send(att.at[0], att.at[1], dev_core, r_a)

    lax.fori_loop(1, 2, back_z, 0)
    zs[0] = dk[0].astype(BF)
    zs[1] = dv[0].astype(BF)
    send(zs, zr, dev_z, r_zb)

    arrived(g2.at[1], r_gx)
    pltpu.make_async_copy(g_in.at[:, hc], g2.at[0], lsem.at[l_h]).wait()
    arrived(att.at[1], r_a)

    def term(n, _):
        wide = pl.ds(pl.multiple_of(n * 256, 256), 256)
        d = dot_tn(att[...].reshape(2 * TILE, FEAT), g2[:, :, wide].reshape(2 * TILE, 256))
        for h in range(2):
            for xx in range(4):
                part = d[h * 256 + xx * 64 :][:64]
                acc[xx, h, :, wide] = part
                xs[xx, h, :, wide] = part.astype(BF)
        return 0

    two, rows = pl.ds(0, 2), pl.ds(0, 64)
    eighth = QUART // 2
    r_xa, r_xr = new("r", 4), new("r", 8)

    def part_a(n):
        return pl.ds(n * QUART, eighth)

    def part_b(n):
        return pl.ds(n * QUART + eighth, eighth)

    def x_first(n):
        send(xs.at[x2_i, two, rows, part_a(n)], xa.at[n, 0], dev_xp, r_xa + 2 * n)
        send(xs.at[x2_i, two, rows, part_b(n)], xa.at[n, 1], dev_xm, r_xa + 2 * n + 1)

    def x_plain(n):
        send(xs.at[xp_i, two, rows, part_b(n)], xr.at[n, 2], dev_xp, r_xr + 4 * n + 2)
        send(xs.at[xm_i, two, rows, part_a(n)], xr.at[n, 3], dev_xm, r_xr + 4 * n + 3)

    def x_second(n):
        arrived(xa.at[n, 0], r_xa + 2 * n)
        xb[n, 0] = (acc[xp_i, :, :, part_a(n)] + xa[n, 0].astype(F32)).astype(BF)
        send(xb.at[n, 0], xr.at[n, 0], dev_xp, r_xr + 4 * n)
        arrived(xa.at[n, 1], r_xa + 2 * n + 1)
        xb[n, 1] = (acc[xm_i, :, :, part_b(n)] + xa[n, 1].astype(F32)).astype(BF)
        send(xb.at[n, 1], xr.at[n, 1], dev_xm, r_xr + 4 * n + 1)

    r_y3, r_y4, r_z4, r_f = new("r", 2), new("r", 2), new("r", 6), new("r", 32)
    half_o = pl.ds(pl.multiple_of((1 - ylo) * eighth, eighth), eighth)
    half_m = pl.ds(pl.multiple_of(ylo * eighth, eighth), eighth)
    mine = pl.ds(pl.multiple_of(z * 16, 16), 16)

    def over_halves(n):
        for r in range(4):
            arrived(xr.at[n, r], r_xr + 4 * n + r)
        for h, (ring, plain) in enumerate(((0, 3), (1, 2))):
            here = pl.ds(h * eighth, eighth)
            there = pl.ds(n * QUART + h * eighth, eighth)
            rsum[n, :, :, here] = (
                acc[x, :, :, there] + xr[n, ring].astype(F32) + xr[n, plain].astype(F32)
            )
        y3s[n] = rsum[n, 1 - yh].astype(BF)
        send(y3s.at[n], y3r.at[n], dev_yi, r_y3 + n)

    def over_row(n):
        arrived(y3r.at[n], r_y3 + n)
        y4s[n] = (rsum[n, yh, :, half_o] + y3r[n, :, half_o].astype(F32)).astype(BF)
        send(y4s.at[n], y4r.at[n], dev_ylo, r_y4 + n)

    def over_rows(n):
        arrived(y4r.at[n], r_y4 + n)
        z4s[n] = (
            rsum[n, yh, :, half_m] + y3r[n, :, half_m].astype(F32) + y4r[n].astype(F32)
        ).astype(BF)
        for k in (1, 2, 3):
            to = lax.rem(z + k, 4)
            some = pl.ds(pl.multiple_of(to * 16, 16), 16)
            send(z4s.at[n, some, pl.ds(0, eighth)], z4r.at[n, k - 1], (dp, to, wa), r_z4 + 3 * n + k - 1)

    places = [
        wgr.at[mine, pl.ds(pl.multiple_of(c * HALF + n * QUART + ylo * eighth, eighth), eighth)]
        for n in range(2)
    ]

    def spread(n):
        total = rsum[n, yh, mine, half_m] + y3r[n, mine, half_m].astype(F32) + y4r[n, mine, :].astype(F32)
        for k in range(3):
            arrived(z4r.at[n, k], r_z4 + 3 * n + k)
            total += z4r[n, k].astype(F32)
        fin[n] = total.astype(BF)
        for k in range(16):
            if k == 0:
                local(fin.at[n], places[n], rsem.at[r_f + 16 * n])
            else:
                dev = (dp, lax.rem(z + k // 4, 4), lax.rem(wa + k % 4, 4))
                send(fin.at[n], places[n], dev, r_f + 16 * n + k)

    lax.fori_loop(0, 3, term, 0)
    x_first(0)
    x_plain(0)
    lax.fori_loop(3, 6, term, 0)
    x_first(1)

    r_dq, r_dk, r_dv = new("r", 4), new("r", 4), new("r", 4)
    b_far, b_near = 2 - i, 1 + i

    def back_far(n, _):
        back(n, b_far)
        return 0

    def give(buf, into, r, n):
        if n:
            send(buf.at[peer_t[n]], into.at[:, cols(t_me)], peers[n], r + t_me)
        else:
            local(buf.at[t_me], into.at[:, cols(t_me)], rsem.at[r + t_me])

    def close_keys(b, order):
        for own, buf, sc in ((dk, dkb, SCALE), (dv, dvb, 1.0)):
            buf[pl.ds(2 * (b - 1), 2)] = (own[b] * sc).astype(BF).reshape(2, TILE, HD)
        for n in order:
            give(dkb, dkr, r_dk, n)
            give(dvb, dvr, r_dv, n)

    def near(n):
        t = peer_t[n]
        back(t, b_near)
        dqb[t] = (dq[t] * SCALE).astype(BF)
        give(dqb, dqr, r_dq, n)

    l_o, l_d = new("l", 6), new("l", 4)

    def project(n):
        wide = pl.ds(n * 512, 512)
        oc[:, wide] = dot_nn(att[0], ws[:, :, wide].reshape(FEAT, 512)).astype(BF)
        local(oc.at[:, wide], out_o.at[:, wide], lsem.at[l_o + n])

    lax.fori_loop(0, 3, back_far, 0)
    x_second(0)
    x_plain(1)
    lax.fori_loop(3, 4, back_far, 0)
    near(2)
    x_second(1)
    near(3)
    over_halves(0)

    arrived(cr, r_cb)
    arrived(yr, r_yb)
    arrived(zr, r_zb)
    for n, own in enumerate((dk, dv)):
        own[1, TILE:] += yr[n, :TILE].astype(F32)
        own[2, :TILE] += zr[n, :TILE].astype(F32)
        own[2, TILE:] += (yr[n, TILE:].astype(F32) + zr[n, TILE:].astype(F32)) + cr[n].astype(F32)
    close_keys(b_far, (2, 3))
    near(1)
    over_row(0)
    over_halves(1)
    near(0)
    over_rows(0)
    close_keys(b_near, (1, 0))
    over_row(1)
    project(0)
    spread(0)
    project(1)
    over_rows(1)
    project(2)
    project(3)
    spread(1)
    project(4)
    project(5)

    for n, (r, got) in enumerate(((r_dq, dqr), (r_dk, dkr), (r_dv, dvr))):
        for s in range(4):
            arrived(got.at[:, cols(s)], r + s)
        local(got, (dq_o, dk_o, dv_o)[n], lsem.at[l_d + n])

    for n in range(2):
        for k in range(16):
            arrived(places[n], r_f + 16 * n + k)
    local(wgr, wg_o, lsem.at[l_d + 3])
    for n in range(6):
        wide = pl.ds(n * 512, 512)
        pltpu.make_async_copy(oc.at[:, wide], out_o.at[:, wide], lsem.at[l_o + n]).wait()
    for copy in sends:
        copy.wait_send()
    for n, (got, out) in enumerate(((dqr, dq_o), (dkr, dk_o), (dvr, dv_o), (wgr, wg_o))):
        pltpu.make_async_copy(got, out, lsem.at[l_d + n]).wait()
    assert counts["s"] <= N_SEND and counts["r"] <= N_RECV and counts["l"] <= N_LOCAL, counts


def widen(oi, qi, ki, vi, wi, oo, qo, ko, vo, wo, ov, qv, kv, vv, wv, qf, kf, vf, wf, isem, osem):
    top, low = pl.ds(0, TILE // 2), pl.ds(TILE // 2, TILE // 2)
    halves = [(oi.at[h], ov.at[h], oo.at[h]) for h in (top, low)]
    sets = ((qi, qv, qf, qo), (ki, kv, kf, ko), (vi, vv, vf, vo), (wi, wv, wf, wo))
    for n, (src, mid, _, _) in enumerate(sets):
        pltpu.make_async_copy(src, mid, isem.at[n]).start()
    for n, (src, mid, _) in enumerate(halves):
        pltpu.make_async_copy(src, mid, isem.at[4 + n]).start()
    for n, (src, mid, wide, out) in enumerate(sets):
        pltpu.make_async_copy(src, mid, isem.at[n]).wait()
        wide[...] = mid[...].astype(F32)
        pltpu.make_async_copy(wide, out, osem.at[n]).start()
    for n, (src, mid, out) in enumerate(halves):
        pltpu.make_async_copy(src, mid, isem.at[4 + n]).wait()
        pltpu.make_async_copy(mid, out, osem.at[4 + n]).start()
    for n, (_, _, wide, out) in enumerate(sets):
        pltpu.make_async_copy(wide, out, osem.at[n]).wait()
    for n, (_, mid, out) in enumerate(halves):
        pltpu.make_async_copy(mid, out, osem.at[4 + n]).wait()


def on_device(q, k, v, g, w):
    def vm(*shape, dtype=BF):
        return pltpu.VMEM(shape, dtype)

    def f(*shape):
        return pltpu.VMEM(shape, F32)

    any_spec = pl.BlockSpec(memory_space=pl.ANY)
    tile = jax.ShapeDtypeStruct((TILE, FEAT), BF)
    outs = pl.pallas_call(
        kernel,
        out_shape=(
            jax.ShapeDtypeStruct((TILE, D), BF),
            *[jax.ShapeDtypeStruct((TILE, FEAT), BF)] * 3,
            jax.ShapeDtypeStruct((64, D), BF),
        ),
        in_specs=[any_spec] * 5,
        out_specs=[any_spec] * 5,
        scratch_shapes=[
            vm(4, TILE, HD), vm(9, TILE, HD), vm(9, TILE, 2 * HD),
            f(12, TILE, 2 * TILE), f(TILE, TILE), f(4, TILE, HD),
            vm(12, TILE, 2 * TILE), vm(TILE, TILE), f(4, TILE, 2 * HD),
            f(4, TILE, HD), vm(4, TILE, HD), vm(4, TILE, HD), vm(4, TILE, HD), f(4, TILE, HD),
            f(4, TILE, HD), f(4, 2 * TILE, HD), f(4, 2 * TILE, HD),
            vm(2, 2 * TILE, HD), vm(2, 2 * TILE, HD), vm(2, TILE, HD),
            vm(2, 2 * TILE, HD), vm(2, 2 * TILE, HD), vm(2, TILE, HD),
            vm(4, TILE, HD), vm(4, TILE, HD), vm(4, TILE, HD),
            vm(TILE, FEAT), vm(TILE, FEAT), vm(TILE, FEAT),
            vm(2, TILE, FEAT), vm(TILE, FEAT), f(TILE, FEAT),
            vm(TILE, D), vm(2, TILE, HALF), vm(8, 64, D), vm(TILE, D),
            f(4, 2, 64, HALF), vm(4, 2, 64, HALF),
            vm(2, 2, 2, 64, QUART // 2), vm(2, 2, 2, 64, QUART // 2), vm(2, 4, 2, 64, QUART // 2),
            f(2, 2, 64, QUART), vm(2, 64, QUART), vm(2, 64, QUART),
            vm(2, 64, QUART // 2), vm(2, 64, QUART // 2), vm(2, 64, QUART // 2),
            vm(2, 3, 16, QUART // 2), vm(2, 16, QUART // 2), vm(64, D),
            pltpu.SemaphoreType.DMA((N_SEND,)),
            pltpu.SemaphoreType.DMA((N_RECV,)),
            pltpu.SemaphoreType.DMA((N_LOCAL,)),
        ],
        compiler_params=pltpu.CompilerParams(
            collective_id=0, has_side_effects=True, vmem_limit_bytes=62 << 20
        ),
        name="sublayer",
    )(
        q.reshape(TILE, FEAT), k.reshape(TILE, FEAT), v.reshape(TILE, FEAT), g.reshape(TILE, D), w
    )
    outcome, dq, dk, dv, wg = pl.pallas_call(
        widen,
        out_shape=(
            jax.ShapeDtypeStruct((TILE, D), BF),
            *[jax.ShapeDtypeStruct((TILE, FEAT), F32)] * 3,
            jax.ShapeDtypeStruct((64, D), F32),
        ),
        in_specs=[any_spec] * 5,
        out_specs=[any_spec] * 5,
        scratch_shapes=[
            vm(TILE, D), *[vm(TILE, FEAT)] * 3, vm(64, D), *[f(TILE, FEAT)] * 3, f(64, D),
            pltpu.SemaphoreType.DMA((6,)), pltpu.SemaphoreType.DMA((6,)),
        ],
        compiler_params=pltpu.CompilerParams(vmem_limit_bytes=24 << 20),
        name="widen",
    )(*outs)
    return (
        outcome.reshape(g.shape), dq.reshape(q.shape), dk.reshape(q.shape), dv.reshape(q.shape), wg
    )


def solution(mesh):
    tiles = P("dp", "ha", "wa", None, None)
    return jax.shard_map(
        on_device,
        mesh=mesh,
        in_specs=(tiles, tiles, tiles, tiles, P("dp", None)),
        out_specs=(tiles, tiles, tiles, tiles, P("dp", None)),
        check_vma=False,
    )
```

```python
import math

import jax
import jax.numpy as jnp
from jax import lax
from jax.experimental import pallas as pl
from jax.experimental.pallas import tpu as pltpu
from jax.sharding import PartitionSpec as P

MESH = pl.DeviceIdType.MESH
BF = jnp.bfloat16
F32 = jnp.float32

TILE, HD, FEAT, D = 384, 128, 512, 3072
HALF, QUART = D // 2, D // 4
SCALE = HD**-0.5
EXP_SCALE = SCALE * math.log2(math.e)


def dot_nn(a, b):
    return lax.dot_general(a, b, (((1,), (0,)), ((), ())), preferred_element_type=F32)


def dot_nt(a, b):
    return lax.dot_general(a, b, (((1,), (1,)), ((), ())), preferred_element_type=F32)


def dot_tn(a, b):
    return lax.dot_general(a, b, (((0,), (0,)), ((), ())), preferred_element_type=F32)


def flip(v):
    return v + 1 - 2 * lax.rem(v, 2)


def unit_index(t, b):
    return 3 * t + b - 1 - lax.rem(t, 2) * (1 - lax.div(t, 2))


N_SEND, N_RECV, N_LOCAL = 128, 128, 16


def kernel(
    q_in, k_in, v_in, g_in, w_in,
    out_o, dq_o, dk_o, dv_o, wg_o,
    qg, kg, vg, s_ref, sc_ref, m_ref, p_ref, pc_ref, o_acc, linv, ob, dog, dop, delta,
    dq, dk, dv, ys, zs, cs, yr, zr, cr, dqb, dkb, dvb, dqr, dkr, dvr, att, gat, gat_acc, gov, g2, ws, oc,
    acc, xs, xa, xb, xr, rsum, y3s, y3r, y4s, z4r, fin, wgr,
    ssem, rsem, lsem,
):
    dp, z, wa = lax.axis_index("dp"), lax.axis_index("ha"), lax.axis_index("wa")
    x, yh = lax.rem(dp, 4), lax.div(dp, 4)
    c, ylo = lax.rem(wa, 2), lax.div(wa, 2)
    i, j = lax.rem(lax.div(z + 1, 2), 2), lax.rem(lax.div(wa + 1, 2), 2)
    t_me = 2 * i + j
    zp, wp = flip(z), flip(wa)
    peers = {1: (dp, z, wp), 2: (dp, zp, wa), 3: (dp, zp, wp)}
    peer_t = {0: t_me, 1: 2 * i + 1 - j, 2: 2 * (1 - i) + j, 3: 2 * (1 - i) + 1 - j}
    dev_y, dev_z, dev_c = (dp, z, 3 - wa), (dp, 3 - z, wa), (dp, 3 - z, 3 - wa)
    xp_i, xm_i, x2_i = lax.rem(x + 1, 4), lax.rem(x + 3, 4), lax.rem(x + 2, 4)
    dev_xp, dev_xm = (yh * 4 + xp_i, z, wa), (yh * 4 + xm_i, z, wa)
    dev_yi = (lax.rem(dp + 4, 8), z, lax.rem(wa + 2, 4))
    dev_core = peers[1]
    dev_ylo = (dp, z, lax.rem(wa + 2, 4))
    clip_devs = [
        (dp, lax.rem(z + a, 4), lax.rem(wa + b, 4)) for a in range(4) for b in range(4) if a or b
    ]
    fl = 4 * (1 - yh)

    sends = []
    counts = {"s": 0, "r": 0, "l": 0}

    def new(kind, n=1):
        first = counts[kind]
        counts[kind] += n
        return first

    def send(src, dst, dev, r):
        copy = pltpu.make_async_remote_copy(
            src, dst, ssem.at[new("s")], rsem.at[r], device_id=dev, device_id_type=MESH
        )
        copy.start()
        sends.append(copy)

    def local(src, dst, sem):
        pltpu.make_async_copy(src, dst, sem).start()

    def arrived(dst, r):
        pltpu.make_async_copy(dst, dst, rsem.at[r]).wait()

    def cols(n, width=HD):
        return pl.ds(pl.multiple_of(n * width, width), width)

    barrier = pltpu.get_barrier_semaphore()
    neighbours = clip_devs + [dev_xp, dev_xm, dev_yi]
    for dev in neighbours:
        pl.semaphore_signal(barrier, inc=1, device_id=dev, device_id_type=MESH)

    l_g, l_w = new("l"), new("l")
    local(g_in, gov, lsem.at[l_g])
    l_h = new("l")
    local(g_in.at[:, pl.ds(pl.multiple_of(c * HALF, HALF), HALF)], g2.at[0], lsem.at[l_h])
    local(w_in, ws.at[dp], lsem.at[l_w])
    r_k, r_q, r_v = new("r", 4), new("r", 4), new("r", 4)
    local(k_in.at[:, cols(t_me)], kg.at[2 + t_me], rsem.at[r_k + t_me])
    local(q_in.at[:, cols(t_me)], qg.at[t_me], rsem.at[r_q + t_me])
    local(v_in.at[:, cols(t_me)], vg.at[2 + t_me, :, pl.ds(0, HD)], rsem.at[r_v + t_me])
    pl.semaphore_wait(barrier, len(neighbours))

    for n in (2, 3, 1):
        send(k_in.at[:, cols(peer_t[n])], kg.at[2 + t_me], peers[n], r_k + t_me)
    hc = pl.ds(pl.multiple_of(c * HALF, HALF), HALF)
    hca = pl.ds(pl.multiple_of(c * HALF, HALF), QUART)
    hcb = pl.ds(pl.multiple_of(c * HALF + QUART, QUART), QUART)
    hall = pl.ds(0, 64)
    r_w = new("r", 8)
    r_wc = new("r", 7)
    send(w_in.at[hall, hc], ws.at[dp, hall, hc], dev_xp, r_w + 0)
    send(w_in.at[hall, hc], ws.at[dp, hall, hc], dev_xm, r_w + 1)
    send(w_in.at[hall, hc], ws.at[dp, hall, hc], dev_yi, r_w + 2)
    for n in (2, 3, 1):
        send(q_in.at[:, cols(peer_t[n])], qg.at[t_me], peers[n], r_q + t_me)
    for n in (2, 3, 1):
        send(v_in.at[:, cols(peer_t[n])], vg.at[2 + t_me, :, pl.ds(0, HD)], peers[n], r_v + t_me)

    r_gx = new("r")
    hc_o = pl.ds(pl.multiple_of((1 - c) * HALF, HALF), HALF)
    send(g_in.at[:, hc_o], g2.at[1], dev_core, r_gx)

    def ones(s, _):
        vg[s, :, HD:] = jnp.ones((TILE, HD), BF)
        return 0

    lax.fori_loop(0, 9, ones, 0)
    m_ref[...] = jnp.full(m_ref.shape, -jnp.inf, F32)
    dq[...] = jnp.zeros(dq.shape, F32)
    dk[...] = jnp.zeros(dk.shape, F32)
    dv[...] = jnp.zeros(dv.shape, F32)
    o_acc[...] = jnp.zeros(o_acc.shape, F32)

    def halo_of(buf, r_own, width, r_halo):
        def at(s):
            return buf.at[s] if width is None else buf.at[s, :, pl.ds(0, width)]

        for s in (3, 5, 4, 2):
            arrived(at(s), r_own + s - 2)
            if s == 3:
                send(at(3), at(6), dev_y, r_halo + 2)
            if s == 5:
                send(at(5), at(7), dev_y, r_halo + 3)
                send(at(5), at(1), dev_z, r_halo + 1)
                send(at(5), at(8), dev_c, r_halo + 4)
            if s == 4:
                send(at(4), at(0), dev_z, r_halo + 0)

    def w_at(d, columns):
        return ws.at[d, hall, columns]

    d_xm, d_xp, d_x2 = yh * 4 + xm_i, yh * 4 + xp_i, yh * 4 + x2_i
    f_x, f_xm, f_xp, f_x2 = fl + x, fl + xm_i, fl + xp_i, fl + x2_i

    r_kh, r_vh = new("r", 5), new("r", 5)
    halo_of(kg, r_k, None, r_kh)

    arrived(w_at(d_xm, hc), r_w + 0)
    send(w_at(d_xm, hca), w_at(d_xm, hca), dev_xp, r_w + 3)
    send(w_at(d_xm, hc), w_at(d_xm, hc), dev_core, r_wc + 0)
    arrived(w_at(d_xp, hc), r_w + 1)
    send(w_at(d_xp, hcb), w_at(d_xp, hcb), dev_xm, r_w + 4)
    send(w_at(d_xp, hc), w_at(d_xp, hc), dev_core, r_wc + 1)
    arrived(w_at(f_x, hc), r_w + 2)
    send(w_at(f_x, hc), w_at(f_x, hc), dev_xp, r_w + 5)
    send(w_at(f_x, hc), w_at(f_x, hc), dev_xm, r_w + 6)
    send(w_at(f_x, hc), w_at(f_x, hc), dev_core, r_wc + 2)

    for s in range(4):
        arrived(qg.at[s], r_q + s)
    arrived(w_at(d_x2, hca), r_w + 3)
    arrived(w_at(d_x2, hcb), r_w + 4)
    send(w_at(d_x2, hc), w_at(d_x2, hc), dev_yi, r_w + 7)
    send(w_at(d_x2, hc), w_at(d_x2, hc), dev_core, r_wc + 3)

    def scores(t, b):
        s = dot_nt(qg[t], kg[pl.ds(2 * b, 2)].reshape(2 * TILE, HD))
        s_ref[unit_index(t, b)] = s
        m = m_ref[t]
        for n in range(6):
            m = jnp.maximum(m, s[:, n * HD : (n + 1) * HD])
        m_ref[t] = m

    def own_scores(n, _):
        scores(lax.div(n, 2), 1 + lax.rem(n, 2))
        return 0

    lax.fori_loop(0, 8, own_scores, 0)

    for s, r in ((0, 0), (1, 1), (6, 2), (7, 3), (8, 4)):
        arrived(kg.at[s], r_kh + r)

    def halo_scores(n, _):
        late = lax.div(n, 2)
        scores(jnp.where(late == 0, 1 + 2 * n, n), 3 - 3 * late)
        return 0

    lax.fori_loop(0, 4, halo_scores, 0)
    s = dot_nt(qg[3], kg[8])
    sc_ref[...] = s
    m_ref[3] = jnp.maximum(
        jnp.maximum(m_ref[3], s[:, :HD]), jnp.maximum(s[:, HD : 2 * HD], s[:, 2 * HD :])
    )

    halo_of(vg, r_v, HD, r_vh)

    arrived(w_at(f_xm, hc), r_w + 5)
    send(w_at(f_xm, hc), w_at(f_xm, hc), dev_core, r_wc + 4)
    arrived(w_at(f_xp, hc), r_w + 6)
    send(w_at(f_xp, hc), w_at(f_xp, hc), dev_core, r_wc + 5)

    def row_max(t, _):
        m = jnp.max(m_ref[t], axis=-1, keepdims=True) * EXP_SCALE
        m_ref[t] = jnp.broadcast_to(m, (TILE, HD))
        return 0

    lax.fori_loop(0, 4, row_max, 0)

    def weigh(t, b):
        u = unit_index(t, b)
        p = jnp.exp2(s_ref[u] * EXP_SCALE - m_ref[t][:, :1]).astype(BF)
        p_ref[u] = p
        o_acc[t] += dot_nn(p, vg[pl.ds(2 * b, 2)].reshape(2 * TILE, 2 * HD))

    def weigh_own(n, _):
        weigh(lax.div(n, 2), 1 + lax.rem(n, 2))
        return 0

    lax.fori_loop(0, 4, weigh_own, 0)
    arrived(w_at(f_x2, hc), r_w + 7)
    send(w_at(f_x2, hc), w_at(f_x2, hc), dev_core, r_wc + 6)
    lax.fori_loop(4, 6, weigh_own, 0)

    pltpu.make_async_copy(g_in, gov, lsem.at[l_g]).wait()
    pltpu.make_async_copy(w_in, ws.at[dp], lsem.at[l_w]).wait()
    for n, d in enumerate((d_xm, d_xp, f_x, d_x2, f_xm, f_xp, f_x2)):
        arrived(w_at(d, hc_o), r_wc + n)
    gat_acc[...] = jnp.zeros(gat_acc.shape, F32)

    def grad_block(n, _):
        wide = pl.ds(pl.multiple_of(n * 512, 512), 512)
        gat_acc[...] += dot_nt(gov[:, wide], ws[:, :, wide].reshape(FEAT, 512))
        return 0

    lax.fori_loop(0, 6, grad_block, 0)
    gat[...] = gat_acc[...].astype(BF)
    r_g = new("r", 4)
    for n in (2, 3, 1):
        send(gat.at[:, cols(peer_t[n])], dog.at[t_me], peers[n], r_g + t_me)
    local(gat.at[:, cols(t_me)], dog.at[t_me], rsem.at[r_g + t_me])

    lax.fori_loop(6, 8, weigh_own, 0)
    for s, r in ((0, 0), (1, 1), (6, 2), (7, 3), (8, 4)):
        arrived(vg.at[s, :, pl.ds(0, HD)], r_vh + r)

    def weigh_halo(n, _):
        late = lax.div(n, 2)
        weigh(jnp.where(late == 0, 1 + 2 * n, n), 3 - 3 * late)
        return 0

    lax.fori_loop(0, 4, weigh_halo, 0)
    p = jnp.exp2(sc_ref[...] * EXP_SCALE - m_ref[3][:, :1]).astype(BF)
    pc_ref[...] = p
    o_acc[3] += dot_nn(p, vg[8])

    r_o = new("r", 4)
    for n in (2, 3, 1, 0):
        t = peer_t[n]
        inverse = 1.0 / o_acc[t, :, HD:]
        linv[t] = inverse
        ob[t] = (o_acc[t, :, :HD] * inverse).astype(BF)
        if n:
            send(ob.at[t], att.at[0, :, cols(t_me)], peers[n], r_o + t_me)
        else:
            local(ob.at[t], att.at[0, :, cols(t_me)], rsem.at[r_o + t_me])

    for s in range(4):
        arrived(dog.at[s], r_g + s)

    def prepare(t, _):
        scaled = (dog[t].astype(F32) * linv[t]).astype(BF)
        dop[t] = scaled
        d = jnp.sum(ob[t].astype(F32) * scaled.astype(F32), axis=-1, keepdims=True)
        delta[t] = jnp.broadcast_to(d, (TILE, HD))
        return 0

    lax.fori_loop(0, 4, prepare, 0)

    def back(t, b):
        p = p_ref[unit_index(t, b)]
        keys = kg[pl.ds(2 * b, 2)].reshape(2 * TILE, HD)
        values = vg[pl.ds(2 * b, 2), :, :HD].reshape(2 * TILE, HD)
        dprob = dot_nt(dop[t], values)
        ds = (p.astype(F32) * (dprob - delta[t][:, :1])).astype(BF)
        dq[t] += dot_nn(ds, keys)
        dk[b] += dot_tn(ds, qg[t])
        dv[b] += dot_tn(p, dop[t])

    def back_y(n, _):
        back(1 + 2 * n, jnp.int32(3))
        return 0

    def back_z(n, _):
        back(2 + n, jnp.int32(0))
        return 0

    r_cb, r_yb, r_zb = new("r", 2), new("r", 2), new("r", 2)
    p = pc_ref[...]
    dprob = dot_nt(dop[3], vg[8, :, :HD])
    ds = (p.astype(F32) * (dprob - delta[3][:, :1])).astype(BF)
    dq[3] += dot_nn(ds, kg[8])
    cs[0] = dot_tn(ds, qg[3]).astype(BF)
    cs[1] = dot_tn(p, dop[3]).astype(BF)
    send(cs.at[0], cr.at[0], dev_c, r_cb)

    lax.fori_loop(0, 2, back_y, 0)
    ys[0] = dk[3].astype(BF)
    ys[1] = dv[3].astype(BF)
    for n in range(2):
        send(ys.at[n], yr.at[n], dev_y, r_yb + n)
    lax.fori_loop(0, 1, back_z, 0)

    for s in range(4):
        arrived(att.at[0, :, cols(s)], r_o + s)
    r_a = new("r")
    send(att.at[0], att.at[1], dev_core, r_a)

    lax.fori_loop(1, 2, back_z, 0)
    zs[0] = dk[0].astype(BF)
    zs[1] = dv[0].astype(BF)
    for n in range(2):
        send(zs.at[n], zr.at[n], dev_z, r_zb + n)
    send(cs.at[1], cr.at[1], dev_c, r_cb + 1)

    arrived(g2.at[1], r_gx)
    pltpu.make_async_copy(g_in.at[:, hc], g2.at[0], lsem.at[l_h]).wait()
    arrived(att.at[1], r_a)

    def term(n, _):
        wide = pl.ds(pl.multiple_of(n * 256, 256), 256)
        d = dot_tn(att[...].reshape(2 * TILE, FEAT), g2[:, :, wide].reshape(2 * TILE, 256))
        for h in range(2):
            for xx in range(4):
                part = d[h * 256 + xx * 64 :][:64]
                acc[xx, h, :, wide] = part
                xs[xx, h, :, wide] = part.astype(BF)
        return 0

    two, rows = pl.ds(0, 2), pl.ds(0, 64)
    eighth = QUART // 2
    r_xa, r_xr = new("r", 4), new("r", 8)

    def part_a(n):
        return pl.ds(n * QUART, eighth)

    def part_b(n):
        return pl.ds(n * QUART + eighth, eighth)

    def x_first(n):
        send(xs.at[x2_i, two, rows, part_a(n)], xa.at[n, 0], dev_xp, r_xa + 2 * n)
        send(xs.at[x2_i, two, rows, part_b(n)], xa.at[n, 1], dev_xm, r_xa + 2 * n + 1)

    def x_plain(n):
        send(xs.at[xp_i, two, rows, part_b(n)], xr.at[n, 2], dev_xp, r_xr + 4 * n + 2)
        send(xs.at[xm_i, two, rows, part_a(n)], xr.at[n, 3], dev_xm, r_xr + 4 * n + 3)

    def x_second(n):
        arrived(xa.at[n, 0], r_xa + 2 * n)
        xb[n, 0] = (acc[xp_i, :, :, part_a(n)] + xa[n, 0].astype(F32)).astype(BF)
        send(xb.at[n, 0], xr.at[n, 0], dev_xp, r_xr + 4 * n)
        arrived(xa.at[n, 1], r_xa + 2 * n + 1)
        xb[n, 1] = (acc[xm_i, :, :, part_b(n)] + xa[n, 1].astype(F32)).astype(BF)
        send(xb.at[n, 1], xr.at[n, 1], dev_xm, r_xr + 4 * n + 1)

    r_y3, r_z4, r_f = new("r", 2), new("r", 14), new("r", 32)
    half_m = pl.ds(pl.multiple_of(ylo * eighth, eighth), eighth)
    mine = pl.ds(pl.multiple_of(z * 16, 16), 16)

    def over_halves(n):
        for r in range(4):
            arrived(xr.at[n, r], r_xr + 4 * n + r)
        for h, (ring, plain) in enumerate(((0, 3), (1, 2))):
            here = pl.ds(h * eighth, eighth)
            there = pl.ds(n * QUART + h * eighth, eighth)
            rsum[n, :, :, here] = (
                acc[x, :, :, there] + xr[n, ring].astype(F32) + xr[n, plain].astype(F32)
            )
        y3s[n] = rsum[n, 1 - yh].astype(BF)
        send(y3s.at[n], y3r.at[n], dev_yi, r_y3 + n)

    def over_row(n):
        arrived(y3r.at[n], r_y3 + n)
        y4s[n] = (rsum[n, yh] + y3r[n].astype(F32)).astype(BF)
        for k in range(1, 8):
            to_z, to_y = lax.rem(z + k // 2, 4), lax.rem(ylo + k % 2, 2)
            some = pl.ds(pl.multiple_of(to_z * 16, 16), 16)
            part = pl.ds(pl.multiple_of(to_y * eighth, eighth), eighth)
            send(y4s.at[n, some, part], z4r.at[n, k - 1], (dp, to_z, 2 * to_y + c), r_z4 + 7 * n + k - 1)

    places = [
        wgr.at[mine, pl.ds(pl.multiple_of(c * HALF + n * QUART + ylo * eighth, eighth), eighth)]
        for n in range(2)
    ]

    def spread(n):
        total = rsum[n, yh, mine, half_m] + y3r[n, mine, half_m].astype(F32)
        for k in range(7):
            arrived(z4r.at[n, k], r_z4 + 7 * n + k)
            total += z4r[n, k].astype(F32)
        fin[n] = total.astype(BF)
        for k in range(16):
            if k == 0:
                local(fin.at[n], places[n], rsem.at[r_f + 16 * n])
            else:
                dev = (dp, lax.rem(z + k // 4, 4), lax.rem(wa + k % 4, 4))
                send(fin.at[n], places[n], dev, r_f + 16 * n + k)

    lax.fori_loop(0, 3, term, 0)
    x_first(0)
    x_plain(0)
    lax.fori_loop(3, 6, term, 0)
    x_first(1)

    r_dq, r_dk, r_dv = new("r", 4), new("r", 4), new("r", 4)
    b_far, b_near = 2 - i, 1 + i

    def back_far(n, _):
        back(n, b_far)
        return 0

    def give(buf, into, r, n):
        if n:
            send(buf.at[peer_t[n]], into.at[:, cols(t_me)], peers[n], r + t_me)
        else:
            local(buf.at[t_me], into.at[:, cols(t_me)], rsem.at[r + t_me])

    def add_neighbours(n):
        own = (dk, dv)[n]
        for buf, r in ((cr, r_cb), (yr, r_yb), (zr, r_zb)):
            arrived(buf.at[n], r + n)
        own[1, TILE:] += yr[n, :TILE].astype(F32)
        own[2, :TILE] += zr[n, :TILE].astype(F32)
        own[2, TILE:] += (yr[n, TILE:].astype(F32) + zr[n, TILE:].astype(F32)) + cr[n].astype(F32)

    def close_keys(n, b, order):
        own, buf, into, r, sc = ((dk, dkb, dkr, r_dk, SCALE), (dv, dvb, dvr, r_dv, 1.0))[n]
        buf[pl.ds(2 * (b - 1), 2)] = (own[b] * sc).astype(BF).reshape(2, TILE, HD)
        for k in order:
            give(buf, into, r, k)

    def near(n):
        t = peer_t[n]
        back(t, b_near)
        dqb[t] = (dq[t] * SCALE).astype(BF)
        give(dqb, dqr, r_dq, n)

    l_o, l_d = new("l", 6), new("l", 4)

    def project(n):
        wide = pl.ds(n * 512, 512)
        oc[:, wide] = dot_nn(att[0], ws[:, :, wide].reshape(FEAT, 512)).astype(BF)
        local(oc.at[:, wide], out_o.at[:, wide], lsem.at[l_o + n])

    lax.fori_loop(0, 3, back_far, 0)
    x_second(0)
    x_plain(1)
    lax.fori_loop(3, 4, back_far, 0)
    near(2)
    x_second(1)
    add_neighbours(0)
    close_keys(0, b_far, (2, 3))
    near(3)
    over_halves(0)
    near(1)
    add_neighbours(1)
    close_keys(1, b_far, (2, 3))
    over_row(0)
    over_halves(1)
    near(0)
    close_keys(0, b_near, (1, 0))
    close_keys(1, b_near, (1, 0))
    spread(0)
    project(0)
    over_row(1)
    for n in range(1, 6):
        project(n)
    spread(1)

    for n, (r, got) in enumerate(((r_dq, dqr), (r_dk, dkr), (r_dv, dvr))):
        for s in range(4):
            arrived(got.at[:, cols(s)], r + s)
        local(got, (dq_o, dk_o, dv_o)[n], lsem.at[l_d + n])

    for n in range(2):
        for k in range(16):
            arrived(places[n], r_f + 16 * n + k)
    local(wgr, wg_o, lsem.at[l_d + 3])
    for n in range(6):
        wide = pl.ds(n * 512, 512)
        pltpu.make_async_copy(oc.at[:, wide], out_o.at[:, wide], lsem.at[l_o + n]).wait()
    for copy in sends:
        copy.wait_send()
    for n, (got, out) in enumerate(((dqr, dq_o), (dkr, dk_o), (dvr, dv_o), (wgr, wg_o))):
        pltpu.make_async_copy(got, out, lsem.at[l_d + n]).wait()
    assert counts["s"] <= N_SEND and counts["r"] <= N_RECV and counts["l"] <= N_LOCAL, counts


def widen(oi, qi, ki, vi, wi, oo, qo, ko, vo, wo, ov, qv, kv, vv, wv, qf, kf, vf, wf, isem, osem):
    top, low = pl.ds(0, TILE // 2), pl.ds(TILE // 2, TILE // 2)
    halves = [(oi.at[h], ov.at[h], oo.at[h]) for h in (top, low)]
    sets = ((qi, qv, qf, qo), (ki, kv, kf, ko), (vi, vv, vf, vo), (wi, wv, wf, wo))
    for n, (src, mid, _, _) in enumerate(sets):
        pltpu.make_async_copy(src, mid, isem.at[n]).start()
    for n, (src, mid, _) in enumerate(halves):
        pltpu.make_async_copy(src, mid, isem.at[4 + n]).start()
    for n, (src, mid, wide, out) in enumerate(sets):
        pltpu.make_async_copy(src, mid, isem.at[n]).wait()
        wide[...] = mid[...].astype(F32)
        pltpu.make_async_copy(wide, out, osem.at[n]).start()
    for n, (src, mid, out) in enumerate(halves):
        pltpu.make_async_copy(src, mid, isem.at[4 + n]).wait()
        pltpu.make_async_copy(mid, out, osem.at[4 + n]).start()
    for n, (_, _, wide, out) in enumerate(sets):
        pltpu.make_async_copy(wide, out, osem.at[n]).wait()
    for n, (_, mid, out) in enumerate(halves):
        pltpu.make_async_copy(mid, out, osem.at[4 + n]).wait()


def on_device(q, k, v, g, w):
    def vm(*shape, dtype=BF):
        return pltpu.VMEM(shape, dtype)

    def f(*shape):
        return pltpu.VMEM(shape, F32)

    any_spec = pl.BlockSpec(memory_space=pl.ANY)
    tile = jax.ShapeDtypeStruct((TILE, FEAT), BF)
    outs = pl.pallas_call(
        kernel,
        out_shape=(
            jax.ShapeDtypeStruct((TILE, D), BF),
            *[jax.ShapeDtypeStruct((TILE, FEAT), BF)] * 3,
            jax.ShapeDtypeStruct((64, D), BF),
        ),
        in_specs=[any_spec] * 5,
        out_specs=[any_spec] * 5,
        scratch_shapes=[
            vm(4, TILE, HD), vm(9, TILE, HD), vm(9, TILE, 2 * HD),
            f(12, TILE, 2 * TILE), f(TILE, TILE), f(4, TILE, HD),
            vm(12, TILE, 2 * TILE), vm(TILE, TILE), f(4, TILE, 2 * HD),
            f(4, TILE, HD), vm(4, TILE, HD), vm(4, TILE, HD), vm(4, TILE, HD), f(4, TILE, HD),
            f(4, TILE, HD), f(4, 2 * TILE, HD), f(4, 2 * TILE, HD),
            vm(2, 2 * TILE, HD), vm(2, 2 * TILE, HD), vm(2, TILE, HD),
            vm(2, 2 * TILE, HD), vm(2, 2 * TILE, HD), vm(2, TILE, HD),
            vm(4, TILE, HD), vm(4, TILE, HD), vm(4, TILE, HD),
            vm(TILE, FEAT), vm(TILE, FEAT), vm(TILE, FEAT),
            vm(2, TILE, FEAT), vm(TILE, FEAT), f(TILE, FEAT),
            vm(TILE, D), vm(2, TILE, HALF), vm(8, 64, D), vm(TILE, D),
            f(4, 2, 64, HALF), vm(4, 2, 64, HALF),
            vm(2, 2, 2, 64, QUART // 2), vm(2, 2, 2, 64, QUART // 2), vm(2, 4, 2, 64, QUART // 2),
            f(2, 2, 64, QUART), vm(2, 64, QUART), vm(2, 64, QUART),
            vm(2, 64, QUART),
            vm(2, 7, 16, QUART // 2), vm(2, 16, QUART // 2), vm(64, D),
            pltpu.SemaphoreType.DMA((N_SEND,)),
            pltpu.SemaphoreType.DMA((N_RECV,)),
            pltpu.SemaphoreType.DMA((N_LOCAL,)),
        ],
        compiler_params=pltpu.CompilerParams(
            collective_id=0, has_side_effects=True, vmem_limit_bytes=62 << 20
        ),
        name="sublayer",
    )(
        q.reshape(TILE, FEAT), k.reshape(TILE, FEAT), v.reshape(TILE, FEAT), g.reshape(TILE, D), w
    )
    outcome, dq, dk, dv, wg = pl.pallas_call(
        widen,
        out_shape=(
            jax.ShapeDtypeStruct((TILE, D), BF),
            *[jax.ShapeDtypeStruct((TILE, FEAT), F32)] * 3,
            jax.ShapeDtypeStruct((64, D), F32),
        ),
        in_specs=[any_spec] * 5,
        out_specs=[any_spec] * 5,
        scratch_shapes=[
            vm(TILE, D), *[vm(TILE, FEAT)] * 3, vm(64, D), *[f(TILE, FEAT)] * 3, f(64, D),
            pltpu.SemaphoreType.DMA((6,)), pltpu.SemaphoreType.DMA((6,)),
        ],
        compiler_params=pltpu.CompilerParams(vmem_limit_bytes=62 << 20),
        name="widen",
    )(*outs)
    return (
        outcome.reshape(g.shape), dq.reshape(q.shape), dk.reshape(q.shape), dv.reshape(q.shape), wg
    )


def solution(mesh):
    tiles = P("dp", "ha", "wa", None, None)
    return jax.shard_map(
        on_device,
        mesh=mesh,
        in_specs=(tiles, tiles, tiles, tiles, P("dp", None)),
        out_specs=(tiles, tiles, tiles, tiles, P("dp", None)),
        check_vma=False,
    )
```

```python
import math

import jax
import jax.numpy as jnp
from jax import lax
from jax.experimental import pallas as pl
from jax.experimental.pallas import tpu as pltpu
from jax.sharding import PartitionSpec as P

MESH = pl.DeviceIdType.MESH
BF = jnp.bfloat16
F32 = jnp.float32

TILE, HD, FEAT, D = 384, 128, 512, 3072
HALF, QUART = D // 2, D // 4
SCALE = HD**-0.5
EXP_SCALE = SCALE * math.log2(math.e)


def dot_nn(a, b):
    return lax.dot_general(a, b, (((1,), (0,)), ((), ())), preferred_element_type=F32)


def dot_nt(a, b):
    return lax.dot_general(a, b, (((1,), (1,)), ((), ())), preferred_element_type=F32)


def dot_tn(a, b):
    return lax.dot_general(a, b, (((0,), (0,)), ((), ())), preferred_element_type=F32)


def flip(v):
    return v + 1 - 2 * lax.rem(v, 2)


def unit_index(t, b):
    return 3 * t + b - 1 - lax.rem(t, 2) * (1 - lax.div(t, 2))


N_SEND, N_RECV, N_LOCAL = 128, 128, 16


def kernel(
    q_in, k_in, v_in, g_in, w_in,
    out_o, dq_o, dk_o, dv_o, wg_o,
    qg, kg, vg, s_ref, sc_ref, m_ref, p_ref, pc_ref, o_acc, linv, ob, dog, dop, delta,
    dq, dk, dv, ys, zs, cs, yr, zr, cr, dqb, dkb, dvb, dqr, dkr, dvr, att, gat, gat_acc, gov, g2, ws, oc,
    acc, xs, xa, xb, xr, rsum, y3s, y3r, y4s, z4r, fin, wgr,
    ssem, rsem, lsem,
):
    dp, z, wa = lax.axis_index("dp"), lax.axis_index("ha"), lax.axis_index("wa")
    x, yh = lax.rem(dp, 4), lax.div(dp, 4)
    c, ylo = lax.rem(wa, 2), lax.div(wa, 2)
    i, j = lax.rem(lax.div(z + 1, 2), 2), lax.rem(lax.div(wa + 1, 2), 2)
    t_me = 2 * i + j
    zp, wp = flip(z), flip(wa)
    peers = {1: (dp, z, wp), 2: (dp, zp, wa), 3: (dp, zp, wp)}
    peer_t = {0: t_me, 1: 2 * i + 1 - j, 2: 2 * (1 - i) + j, 3: 2 * (1 - i) + 1 - j}
    dev_y, dev_z, dev_c = (dp, z, 3 - wa), (dp, 3 - z, wa), (dp, 3 - z, 3 - wa)
    xp_i, xm_i, x2_i = lax.rem(x + 1, 4), lax.rem(x + 3, 4), lax.rem(x + 2, 4)
    dev_xp, dev_xm = (yh * 4 + xp_i, z, wa), (yh * 4 + xm_i, z, wa)
    dev_yi = (lax.rem(dp + 4, 8), z, lax.rem(wa + 2, 4))
    dev_core = peers[1]
    dev_ylo = (dp, z, lax.rem(wa + 2, 4))
    clip_devs = [
        (dp, lax.rem(z + a, 4), lax.rem(wa + b, 4)) for a in range(4) for b in range(4) if a or b
    ]
    fl = 4 * (1 - yh)

    sends = []
    counts = {"s": 0, "r": 0, "l": 0}

    def new(kind, n=1):
        first = counts[kind]
        counts[kind] += n
        return first

    def send(src, dst, dev, r):
        copy = pltpu.make_async_remote_copy(
            src, dst, ssem.at[new("s")], rsem.at[r], device_id=dev, device_id_type=MESH
        )
        copy.start()
        sends.append(copy)

    def local(src, dst, sem):
        pltpu.make_async_copy(src, dst, sem).start()

    def arrived(dst, r):
        pltpu.make_async_copy(dst, dst, rsem.at[r]).wait()

    def cols(n, width=HD):
        return pl.ds(pl.multiple_of(n * width, width), width)

    barrier = pltpu.get_barrier_semaphore()
    neighbours = clip_devs + [dev_xp, dev_xm, dev_yi]
    for dev in neighbours:
        pl.semaphore_signal(barrier, inc=1, device_id=dev, device_id_type=MESH)

    l_g, l_w = new("l"), new("l")
    local(g_in, gov, lsem.at[l_g])
    l_h = new("l")
    local(g_in.at[:, pl.ds(pl.multiple_of(c * HALF, HALF), HALF)], g2.at[0], lsem.at[l_h])
    local(w_in, ws.at[dp], lsem.at[l_w])
    r_k, r_q, r_v = new("r", 4), new("r", 4), new("r", 4)
    local(k_in.at[:, cols(t_me)], kg.at[2 + t_me], rsem.at[r_k + t_me])
    local(q_in.at[:, cols(t_me)], qg.at[t_me], rsem.at[r_q + t_me])
    local(v_in.at[:, cols(t_me)], vg.at[2 + t_me, :, pl.ds(0, HD)], rsem.at[r_v + t_me])
    pl.semaphore_wait(barrier, len(neighbours))

    for n in (2, 3, 1):
        send(k_in.at[:, cols(peer_t[n])], kg.at[2 + t_me], peers[n], r_k + t_me)
    hc = pl.ds(pl.multiple_of(c * HALF, HALF), HALF)
    hca = pl.ds(pl.multiple_of(c * HALF, HALF), QUART)
    hcb = pl.ds(pl.multiple_of(c * HALF + QUART, QUART), QUART)
    hall = pl.ds(0, 64)
    r_w = new("r", 8)
    r_wc = new("r", 7)
    send(w_in.at[hall, hc], ws.at[dp, hall, hc], dev_xp, r_w + 0)
    send(w_in.at[hall, hc], ws.at[dp, hall, hc], dev_xm, r_w + 1)
    send(w_in.at[hall, hc], ws.at[dp, hall, hc], dev_yi, r_w + 2)
    for n in (2, 3, 1):
        send(q_in.at[:, cols(peer_t[n])], qg.at[t_me], peers[n], r_q + t_me)
    for n in (2, 3, 1):
        send(v_in.at[:, cols(peer_t[n])], vg.at[2 + t_me, :, pl.ds(0, HD)], peers[n], r_v + t_me)

    r_gx = new("r")
    hc_o = pl.ds(pl.multiple_of((1 - c) * HALF, HALF), HALF)
    send(g_in.at[:, hc_o], g2.at[1], dev_core, r_gx)

    def ones(s, _):
        vg[s, :, HD:] = jnp.ones((TILE, HD), BF)
        return 0

    lax.fori_loop(0, 9, ones, 0)
    m_ref[...] = jnp.full(m_ref.shape, -jnp.inf, F32)
    dq[...] = jnp.zeros(dq.shape, F32)
    dk[...] = jnp.zeros(dk.shape, F32)
    dv[...] = jnp.zeros(dv.shape, F32)
    o_acc[...] = jnp.zeros(o_acc.shape, F32)

    def halo_of(buf, r_own, width, r_halo):
        def at(s):
            return buf.at[s] if width is None else buf.at[s, :, pl.ds(0, width)]

        for s in (3, 5, 4, 2):
            arrived(at(s), r_own + s - 2)
            if s == 3:
                send(at(3), at(6), dev_y, r_halo + 2)
            if s == 5:
                send(at(5), at(7), dev_y, r_halo + 3)
                send(at(5), at(1), dev_z, r_halo + 1)
                send(at(5), at(8), dev_c, r_halo + 4)
            if s == 4:
                send(at(4), at(0), dev_z, r_halo + 0)

    def w_at(d, columns):
        return ws.at[d, hall, columns]

    d_xm, d_xp, d_x2 = yh * 4 + xm_i, yh * 4 + xp_i, yh * 4 + x2_i
    f_x, f_xm, f_xp, f_x2 = fl + x, fl + xm_i, fl + xp_i, fl + x2_i

    r_kh, r_vh = new("r", 5), new("r", 5)
    halo_of(kg, r_k, None, r_kh)

    arrived(w_at(d_xm, hc), r_w + 0)
    send(w_at(d_xm, hca), w_at(d_xm, hca), dev_xp, r_w + 3)
    send(w_at(d_xm, hc), w_at(d_xm, hc), dev_core, r_wc + 0)
    arrived(w_at(d_xp, hc), r_w + 1)
    send(w_at(d_xp, hcb), w_at(d_xp, hcb), dev_xm, r_w + 4)
    send(w_at(d_xp, hc), w_at(d_xp, hc), dev_core, r_wc + 1)
    arrived(w_at(f_x, hc), r_w + 2)
    send(w_at(f_x, hc), w_at(f_x, hc), dev_xp, r_w + 5)
    send(w_at(f_x, hc), w_at(f_x, hc), dev_xm, r_w + 6)
    send(w_at(f_x, hc), w_at(f_x, hc), dev_core, r_wc + 2)

    for s in range(4):
        arrived(qg.at[s], r_q + s)
    arrived(w_at(d_x2, hca), r_w + 3)
    arrived(w_at(d_x2, hcb), r_w + 4)
    send(w_at(d_x2, hc), w_at(d_x2, hc), dev_yi, r_w + 7)
    send(w_at(d_x2, hc), w_at(d_x2, hc), dev_core, r_wc + 3)

    def scores(t, b):
        s = dot_nt(qg[t], kg[pl.ds(2 * b, 2)].reshape(2 * TILE, HD))
        s_ref[unit_index(t, b)] = s
        m = m_ref[t]
        for n in range(6):
            m = jnp.maximum(m, s[:, n * HD : (n + 1) * HD])
        m_ref[t] = m

    def own_scores(n, _):
        scores(lax.div(n, 2), 1 + lax.rem(n, 2))
        return 0

    lax.fori_loop(0, 8, own_scores, 0)

    for s, r in ((0, 0), (1, 1), (6, 2), (7, 3), (8, 4)):
        arrived(kg.at[s], r_kh + r)

    def halo_scores(n, _):
        late = lax.div(n, 2)
        scores(jnp.where(late == 0, 1 + 2 * n, n), 3 - 3 * late)
        return 0

    lax.fori_loop(0, 4, halo_scores, 0)
    s = dot_nt(qg[3], kg[8])
    sc_ref[...] = s
    m_ref[3] = jnp.maximum(
        jnp.maximum(m_ref[3], s[:, :HD]), jnp.maximum(s[:, HD : 2 * HD], s[:, 2 * HD :])
    )

    halo_of(vg, r_v, HD, r_vh)

    arrived(w_at(f_xm, hc), r_w + 5)
    send(w_at(f_xm, hc), w_at(f_xm, hc), dev_core, r_wc + 4)
    arrived(w_at(f_xp, hc), r_w + 6)
    send(w_at(f_xp, hc), w_at(f_xp, hc), dev_core, r_wc + 5)

    def row_max(t, _):
        m = jnp.max(m_ref[t], axis=-1, keepdims=True) * EXP_SCALE
        m_ref[t] = jnp.broadcast_to(m, (TILE, HD))
        return 0

    lax.fori_loop(0, 4, row_max, 0)

    def weigh(t, b):
        u = unit_index(t, b)
        p = jnp.exp2(s_ref[u] * EXP_SCALE - m_ref[t][:, :1]).astype(BF)
        p_ref[u] = p
        o_acc[t] += dot_nn(p, vg[pl.ds(2 * b, 2)].reshape(2 * TILE, 2 * HD))

    def weigh_own(n, _):
        weigh(lax.div(n, 2), 1 + lax.rem(n, 2))
        return 0

    lax.fori_loop(0, 4, weigh_own, 0)
    arrived(w_at(f_x2, hc), r_w + 7)
    send(w_at(f_x2, hc), w_at(f_x2, hc), dev_core, r_wc + 6)
    lax.fori_loop(4, 6, weigh_own, 0)

    pltpu.make_async_copy(g_in, gov, lsem.at[l_g]).wait()
    pltpu.make_async_copy(w_in, ws.at[dp], lsem.at[l_w]).wait()
    for n, d in enumerate((d_xm, d_xp, f_x, d_x2, f_xm, f_xp, f_x2)):
        arrived(w_at(d, hc_o), r_wc + n)
    gat_acc[...] = jnp.zeros(gat_acc.shape, F32)

    def grad_block(n, _):
        wide = pl.ds(pl.multiple_of(n * 512, 512), 512)
        gat_acc[...] += dot_nt(gov[:, wide], ws[:, :, wide].reshape(FEAT, 512))
        return 0

    lax.fori_loop(0, 6, grad_block, 0)
    gat[...] = gat_acc[...].astype(BF)
    r_g = new("r", 4)
    for n in (2, 3, 1):
        send(gat.at[:, cols(peer_t[n])], dog.at[t_me], peers[n], r_g + t_me)
    local(gat.at[:, cols(t_me)], dog.at[t_me], rsem.at[r_g + t_me])

    lax.fori_loop(6, 8, weigh_own, 0)
    for s, r in ((0, 0), (1, 1), (6, 2), (7, 3), (8, 4)):
        arrived(vg.at[s, :, pl.ds(0, HD)], r_vh + r)

    def weigh_halo(n, _):
        late = lax.div(n, 2)
        weigh(jnp.where(late == 0, 1 + 2 * n, n), 3 - 3 * late)
        return 0

    lax.fori_loop(0, 4, weigh_halo, 0)
    p = jnp.exp2(sc_ref[...] * EXP_SCALE - m_ref[3][:, :1]).astype(BF)
    pc_ref[...] = p
    o_acc[3] += dot_nn(p, vg[8])

    r_o = new("r", 4)
    for n in (2, 3, 1, 0):
        t = peer_t[n]
        inverse = 1.0 / o_acc[t, :, HD:]
        linv[t] = inverse
        ob[t] = (o_acc[t, :, :HD] * inverse).astype(BF)
        if n:
            send(ob.at[t], att.at[0, :, cols(t_me)], peers[n], r_o + t_me)
        else:
            local(ob.at[t], att.at[0, :, cols(t_me)], rsem.at[r_o + t_me])

    for s in range(4):
        arrived(dog.at[s], r_g + s)

    def prepare(t, _):
        scaled = (dog[t].astype(F32) * linv[t]).astype(BF)
        dop[t] = scaled
        d = jnp.sum(ob[t].astype(F32) * scaled.astype(F32), axis=-1, keepdims=True)
        delta[t] = jnp.broadcast_to(d, (TILE, HD))
        return 0

    lax.fori_loop(0, 4, prepare, 0)

    def back(t, b):
        p = p_ref[unit_index(t, b)]
        keys = kg[pl.ds(2 * b, 2)].reshape(2 * TILE, HD)
        values = vg[pl.ds(2 * b, 2), :, :HD].reshape(2 * TILE, HD)
        dprob = dot_nt(dop[t], values)
        ds = (p.astype(F32) * (dprob - delta[t][:, :1])).astype(BF)
        dq[t] += dot_nn(ds, keys)
        dk[b] += dot_tn(ds, qg[t])
        dv[b] += dot_tn(p, dop[t])

    def back_y(n, _):
        back(1 + 2 * n, jnp.int32(3))
        return 0

    def back_z(n, _):
        back(2 + n, jnp.int32(0))
        return 0

    r_cb, r_yb, r_zb = new("r", 2), new("r", 2), new("r", 2)
    p = pc_ref[...]
    dprob = dot_nt(dop[3], vg[8, :, :HD])
    ds = (p.astype(F32) * (dprob - delta[3][:, :1])).astype(BF)
    dq[3] += dot_nn(ds, kg[8])
    cs[0] = dot_tn(ds, qg[3]).astype(BF)
    cs[1] = dot_tn(p, dop[3]).astype(BF)
    send(cs.at[0], cr.at[0], dev_c, r_cb)

    lax.fori_loop(0, 2, back_y, 0)
    ys[0] = dk[3].astype(BF)
    ys[1] = dv[3].astype(BF)
    for n in range(2):
        send(ys.at[n], yr.at[n], dev_y, r_yb + n)
    lax.fori_loop(0, 1, back_z, 0)

    for s in range(4):
        arrived(att.at[0, :, cols(s)], r_o + s)
    r_a = new("r")
    send(att.at[0], att.at[1], dev_core, r_a)


    arrived(g2.at[1], r_gx)
    pltpu.make_async_copy(g_in.at[:, hc], g2.at[0], lsem.at[l_h]).wait()
    arrived(att.at[1], r_a)

    def term(n, _):
        wide = pl.ds(pl.multiple_of(n * 256, 256), 256)
        d = dot_tn(att[...].reshape(2 * TILE, FEAT), g2[:, :, wide].reshape(2 * TILE, 256))
        for h in range(2):
            for xx in range(4):
                part = d[h * 256 + xx * 64 :][:64]
                acc[xx, h, :, wide] = part
                xs[xx, h, :, wide] = part.astype(BF)
        return 0

    two, rows = pl.ds(0, 2), pl.ds(0, 64)
    eighth = QUART // 2
    r_xa, r_xr = new("r", 4), new("r", 8)

    def part_a(n):
        return pl.ds(n * QUART, eighth)

    def part_b(n):
        return pl.ds(n * QUART + eighth, eighth)

    def x_first(n):
        send(xs.at[x2_i, two, rows, part_a(n)], xa.at[n, 0], dev_xp, r_xa + 2 * n)
        send(xs.at[x2_i, two, rows, part_b(n)], xa.at[n, 1], dev_xm, r_xa + 2 * n + 1)

    def x_plain(n):
        send(xs.at[xp_i, two, rows, part_b(n)], xr.at[n, 2], dev_xp, r_xr + 4 * n + 2)
        send(xs.at[xm_i, two, rows, part_a(n)], xr.at[n, 3], dev_xm, r_xr + 4 * n + 3)

    def x_second(n):
        arrived(xa.at[n, 0], r_xa + 2 * n)
        xb[n, 0] = (acc[xp_i, :, :, part_a(n)] + xa[n, 0].astype(F32)).astype(BF)
        send(xb.at[n, 0], xr.at[n, 0], dev_xp, r_xr + 4 * n)
        arrived(xa.at[n, 1], r_xa + 2 * n + 1)
        xb[n, 1] = (acc[xm_i, :, :, part_b(n)] + xa[n, 1].astype(F32)).astype(BF)
        send(xb.at[n, 1], xr.at[n, 1], dev_xm, r_xr + 4 * n + 1)

    r_y3, r_z4, r_f = new("r", 2), new("r", 14), new("r", 32)
    half_m = pl.ds(pl.multiple_of(ylo * eighth, eighth), eighth)
    mine = pl.ds(pl.multiple_of(z * 16, 16), 16)

    def over_halves(n):
        for r in range(4):
            arrived(xr.at[n, r], r_xr + 4 * n + r)
        for h, (ring, plain) in enumerate(((0, 3), (1, 2))):
            here = pl.ds(h * eighth, eighth)
            there = pl.ds(n * QUART + h * eighth, eighth)
            rsum[n, :, :, here] = (
                acc[x, :, :, there] + xr[n, ring].astype(F32) + xr[n, plain].astype(F32)
            )
        y3s[n] = rsum[n, 1 - yh].astype(BF)
        send(y3s.at[n], y3r.at[n], dev_yi, r_y3 + n)

    def over_row(n):
        arrived(y3r.at[n], r_y3 + n)
        y4s[n] = (rsum[n, yh] + y3r[n].astype(F32)).astype(BF)
        for k in range(1, 8):
            to_z, to_y = lax.rem(z + k // 2, 4), lax.rem(ylo + k % 2, 2)
            some = pl.ds(pl.multiple_of(to_z * 16, 16), 16)
            part = pl.ds(pl.multiple_of(to_y * eighth, eighth), eighth)
            send(y4s.at[n, some, part], z4r.at[n, k - 1], (dp, to_z, 2 * to_y + c), r_z4 + 7 * n + k - 1)

    places = [
        wgr.at[mine, pl.ds(pl.multiple_of(c * HALF + n * QUART + ylo * eighth, eighth), eighth)]
        for n in range(2)
    ]

    def spread(n):
        total = rsum[n, yh, mine, half_m] + y3r[n, mine, half_m].astype(F32)
        for k in range(7):
            arrived(z4r.at[n, k], r_z4 + 7 * n + k)
            total += z4r[n, k].astype(F32)
        fin[n] = total.astype(BF)
        for k in range(16):
            if k == 0:
                local(fin.at[n], places[n], rsem.at[r_f + 16 * n])
            else:
                dev = (dp, lax.rem(z + k // 4, 4), lax.rem(wa + k % 4, 4))
                send(fin.at[n], places[n], dev, r_f + 16 * n + k)

    lax.fori_loop(0, 3, term, 0)
    x_first(0)
    x_plain(0)
    lax.fori_loop(3, 6, term, 0)
    x_first(1)

    lax.fori_loop(1, 2, back_z, 0)
    zs[0] = dk[0].astype(BF)
    zs[1] = dv[0].astype(BF)
    for n in range(2):
        send(zs.at[n], zr.at[n], dev_z, r_zb + n)
    send(cs.at[1], cr.at[1], dev_c, r_cb + 1)

    r_dq, r_dk, r_dv = new("r", 4), new("r", 4), new("r", 4)
    b_far, b_near = 2 - i, 1 + i

    def back_far(n, _):
        back(n, b_far)
        return 0

    def give(buf, into, r, n):
        if n:
            send(buf.at[peer_t[n]], into.at[:, cols(t_me)], peers[n], r + t_me)
        else:
            local(buf.at[t_me], into.at[:, cols(t_me)], rsem.at[r + t_me])

    def add_neighbours(n):
        own = (dk, dv)[n]
        for buf, r in ((cr, r_cb), (yr, r_yb), (zr, r_zb)):
            arrived(buf.at[n], r + n)
        own[1, TILE:] += yr[n, :TILE].astype(F32)
        own[2, :TILE] += zr[n, :TILE].astype(F32)
        own[2, TILE:] += (yr[n, TILE:].astype(F32) + zr[n, TILE:].astype(F32)) + cr[n].astype(F32)

    def close_keys(n, b, order):
        own, buf, into, r, sc = ((dk, dkb, dkr, r_dk, SCALE), (dv, dvb, dvr, r_dv, 1.0))[n]
        buf[pl.ds(2 * (b - 1), 2)] = (own[b] * sc).astype(BF).reshape(2, TILE, HD)
        for k in order:
            give(buf, into, r, k)

    def near(n):
        t = peer_t[n]
        back(t, b_near)
        dqb[t] = (dq[t] * SCALE).astype(BF)
        give(dqb, dqr, r_dq, n)

    l_o, l_d = new("l", 6), new("l", 4)

    def project(n):
        wide = pl.ds(n * 512, 512)
        oc[:, wide] = dot_nn(att[0], ws[:, :, wide].reshape(FEAT, 512)).astype(BF)
        local(oc.at[:, wide], out_o.at[:, wide], lsem.at[l_o + n])

    lax.fori_loop(0, 2, back_far, 0)
    x_second(0)
    x_plain(1)
    lax.fori_loop(2, 4, back_far, 0)
    x_second(1)
    near(2)
    over_halves(0)
    near(3)
    add_neighbours(0)
    close_keys(0, b_far, (2, 3))
    near(1)
    over_row(0)
    over_halves(1)
    add_neighbours(1)
    close_keys(1, b_far, (2, 3))
    spread(0)
    over_row(1)
    near(0)
    close_keys(0, b_near, (1, 0))
    close_keys(1, b_near, (1, 0))
    spread(1)
    for n in range(6):
        project(n)

    for n, (r, got) in enumerate(((r_dq, dqr), (r_dk, dkr), (r_dv, dvr))):
        for s in range(4):
            arrived(got.at[:, cols(s)], r + s)
        local(got, (dq_o, dk_o, dv_o)[n], lsem.at[l_d + n])

    for n in range(2):
        for k in range(16):
            arrived(places[n], r_f + 16 * n + k)
    local(wgr, wg_o, lsem.at[l_d + 3])
    for n in range(6):
        wide = pl.ds(n * 512, 512)
        pltpu.make_async_copy(oc.at[:, wide], out_o.at[:, wide], lsem.at[l_o + n]).wait()
    for copy in sends:
        copy.wait_send()
    for n, (got, out) in enumerate(((dqr, dq_o), (dkr, dk_o), (dvr, dv_o), (wgr, wg_o))):
        pltpu.make_async_copy(got, out, lsem.at[l_d + n]).wait()
    assert counts["s"] <= N_SEND and counts["r"] <= N_RECV and counts["l"] <= N_LOCAL, counts


def widen(oi, qi, ki, vi, wi, oo, qo, ko, vo, wo, ov, qv, kv, vv, wv, qf, kf, vf, wf, isem, osem):
    top, low = pl.ds(0, TILE // 2), pl.ds(TILE // 2, TILE // 2)
    halves = [(oi.at[h], ov.at[h], oo.at[h]) for h in (top, low)]
    sets = ((qi, qv, qf, qo), (ki, kv, kf, ko), (vi, vv, vf, vo), (wi, wv, wf, wo))
    for n, (src, mid, _, _) in enumerate(sets):
        pltpu.make_async_copy(src, mid, isem.at[n]).start()
    for n, (src, mid, _) in enumerate(halves):
        pltpu.make_async_copy(src, mid, isem.at[4 + n]).start()
    for n, (src, mid, wide, out) in enumerate(sets):
        pltpu.make_async_copy(src, mid, isem.at[n]).wait()
        wide[...] = mid[...].astype(F32)
        pltpu.make_async_copy(wide, out, osem.at[n]).start()
    for n, (src, mid, out) in enumerate(halves):
        pltpu.make_async_copy(src, mid, isem.at[4 + n]).wait()
        pltpu.make_async_copy(mid, out, osem.at[4 + n]).start()
    for n, (_, _, wide, out) in enumerate(sets):
        pltpu.make_async_copy(wide, out, osem.at[n]).wait()
    for n, (_, mid, out) in enumerate(halves):
        pltpu.make_async_copy(mid, out, osem.at[4 + n]).wait()


def on_device(q, k, v, g, w):
    def vm(*shape, dtype=BF):
        return pltpu.VMEM(shape, dtype)

    def f(*shape):
        return pltpu.VMEM(shape, F32)

    any_spec = pl.BlockSpec(memory_space=pl.ANY)
    tile = jax.ShapeDtypeStruct((TILE, FEAT), BF)
    outs = pl.pallas_call(
        kernel,
        out_shape=(
            jax.ShapeDtypeStruct((TILE, D), BF),
            *[jax.ShapeDtypeStruct((TILE, FEAT), BF)] * 3,
            jax.ShapeDtypeStruct((64, D), BF),
        ),
        in_specs=[any_spec] * 5,
        out_specs=[any_spec] * 5,
        scratch_shapes=[
            vm(4, TILE, HD), vm(9, TILE, HD), vm(9, TILE, 2 * HD),
            f(12, TILE, 2 * TILE), f(TILE, TILE), f(4, TILE, HD),
            vm(12, TILE, 2 * TILE), vm(TILE, TILE), f(4, TILE, 2 * HD),
            f(4, TILE, HD), vm(4, TILE, HD), vm(4, TILE, HD), vm(4, TILE, HD), f(4, TILE, HD),
            f(4, TILE, HD), f(4, 2 * TILE, HD), f(4, 2 * TILE, HD),
            vm(2, 2 * TILE, HD), vm(2, 2 * TILE, HD), vm(2, TILE, HD),
            vm(2, 2 * TILE, HD), vm(2, 2 * TILE, HD), vm(2, TILE, HD),
            vm(4, TILE, HD), vm(4, TILE, HD), vm(4, TILE, HD),
            vm(TILE, FEAT), vm(TILE, FEAT), vm(TILE, FEAT),
            vm(2, TILE, FEAT), vm(TILE, FEAT), f(TILE, FEAT),
            vm(TILE, D), vm(2, TILE, HALF), vm(8, 64, D), vm(TILE, D),
            f(4, 2, 64, HALF), vm(4, 2, 64, HALF),
            vm(2, 2, 2, 64, QUART // 2), vm(2, 2, 2, 64, QUART // 2), vm(2, 4, 2, 64, QUART // 2),
            f(2, 2, 64, QUART), vm(2, 64, QUART), vm(2, 64, QUART),
            vm(2, 64, QUART),
            vm(2, 7, 16, QUART // 2), vm(2, 16, QUART // 2), vm(64, D),
            pltpu.SemaphoreType.DMA((N_SEND,)),
            pltpu.SemaphoreType.DMA((N_RECV,)),
            pltpu.SemaphoreType.DMA((N_LOCAL,)),
        ],
        compiler_params=pltpu.CompilerParams(
            collective_id=0, has_side_effects=True, vmem_limit_bytes=62 << 20
        ),
        name="sublayer",
    )(
        q.reshape(TILE, FEAT), k.reshape(TILE, FEAT), v.reshape(TILE, FEAT), g.reshape(TILE, D), w
    )
    outcome, dq, dk, dv, wg = pl.pallas_call(
        widen,
        out_shape=(
            jax.ShapeDtypeStruct((TILE, D), BF),
            *[jax.ShapeDtypeStruct((TILE, FEAT), F32)] * 3,
            jax.ShapeDtypeStruct((64, D), F32),
        ),
        in_specs=[any_spec] * 5,
        out_specs=[any_spec] * 5,
        scratch_shapes=[
            vm(TILE, D), *[vm(TILE, FEAT)] * 3, vm(64, D), *[f(TILE, FEAT)] * 3, f(64, D),
            pltpu.SemaphoreType.DMA((6,)), pltpu.SemaphoreType.DMA((6,)),
        ],
        compiler_params=pltpu.CompilerParams(vmem_limit_bytes=62 << 20),
        name="widen",
    )(*outs)
    return (
        outcome.reshape(g.shape), dq.reshape(q.shape), dk.reshape(q.shape), dv.reshape(q.shape), wg
    )


def solution(mesh):
    tiles = P("dp", "ha", "wa", None, None)
    return jax.shard_map(
        on_device,
        mesh=mesh,
        in_specs=(tiles, tiles, tiles, tiles, P("dp", None)),
        out_specs=(tiles, tiles, tiles, tiles, P("dp", None)),
        check_vma=False,
    )
```
